128 devices in a mesh: seq: 32 (over z, x, core), mp: 4 (over y).
Axes of the slice: x: 4, y: 4, z: 4, core: 2. Of those that a mesh axis runs over, the one named last changes fastest.
Arguments:
- inputs: bfloat16 [4096, 1536], P('seq', 'mp'), may hold values from -6 to 6
- cotangent: bfloat16 [4096, 1536], P('seq', 'mp'), may hold values from -6 to 6
- conv_kernels: bfloat16 [4, 3, 768, 1536], P(None, None, 'mp'), may hold values from -0.09375 to 0.09375
- point_weights: bfloat16 [4, 768, 1536], P(None, 'mp'), may hold values from -0.21875 to 0.21875
Outputs:
- input_grad: float32 [4096, 1536], P('seq', 'mp')
- kernel_grad: float32 [4, 3, 768, 1536], P(None, None, ('mp', 'seq'))
- point_grad: float32 [4, 768, 1536], P(None, ('mp', 'seq'))
The draws below stay inside these ranges and needn't reach their ends.
All inputs are finite; a program needn't handle non-finite values.
Results may differ from the reference program's by a relative error of at most 0.03.
Values may be sent and summed in bfloat16 or wider, within the bound.
No kernel may reach another device: no remote copies, remote signals or barrier semaphores. Data moves between devices by JAX's collectives and lax.ppermute only.
A program may use at most 192 MiB of HBM per device.

```python
import jax
import jax.numpy as jnp

C = 1536
H = 768
LAYERS = 4
POS_DEV = 128
POSITIONS = 4096


def spiked(entries, key, source, target, shards_of, factor):
    owner, partner = [(jnp.arange(entries.shape[position]) // (entries.shape[position] // shards_of)).reshape([-1 if axis == position else 1 for axis in range(entries.ndim)]) for position in (source, target)]
    chosen = jax.random.permutation(key, shards_of)[partner]
    strong = (owner == chosen) | (owner == (partner + shards_of // 2) % shards_of)
    return jnp.where(strong, factor * entries, entries)


def level_of(key, extent, cuts, smallest, high):
    factor_of = 1.0
    for dim, parts in cuts:
        heights = jax.random.uniform(jax.random.fold_in(jax.random.fold_in(key, 6), dim), (parts,), jnp.float32, smallest / len(cuts), high / len(cuts))
        factor_of = factor_of * jnp.repeat(jnp.exp(heights), extent[dim] // parts).reshape((-1,) + (1,) * (len(extent) - 1 - dim))
    return factor_of


def noise(stream_key, shape, scale, limit, shards=(), kind=jnp.bfloat16):
    drawn = jax.random.normal(stream_key, shape, jnp.float32) * scale
    if len(shards) > 0:
        drawn = level_of(stream_key, shape, shards, -0.22, 0.18) * drawn
    return jnp.clip(drawn, min=-limit, max=limit).astype(kind)


def heavy_noise(key, shape, width, most, cuts, heavy, held_as=jnp.bfloat16):
    result = width * jax.random.normal(key, shape, jnp.float32)
    if cuts:
        result = result * level_of(key, shape, cuts, -0.22, 0.18)
    return jnp.clip(spiked(result, jax.random.fold_in(key, 3), *heavy), -most, most).astype(held_as)


def setup_inputs(seed: int = 0) -> dict:
    streams_of = jax.random.split(jax.random.key(seed), 5)
    inputs = noise(streams_of[0], (POSITIONS, C), 1.0, 6.0, ((0, 32), (1, 4)))
    cotangent = heavy_noise(streams_of[1], (POSITIONS, C), 1.0, 6.0, ((0, 32), (1, 4)), (0, 1, 32, 2.75))
    conv_kernels = noise(streams_of[2], (LAYERS, 3, H, C), (3 * C) ** -0.5, 0.09375, ((2, 4),))
    point_weights = noise(streams_of[3], (LAYERS, H, C), H ** -0.5, 0.21875, ((1, 4),))
    return {"inputs": inputs, "cotangent": cotangent, "conv_kernels": conv_kernels, "point_weights": point_weights}


def gelu_slope(values):
    return jax.vjp(jax.nn.gelu, values)[1](jnp.ones_like(values))[0]

def moved(values, offset):
    margin = abs(offset)
    padded = jnp.pad(values, ((margin, margin), (0, 0)))
    return padded[margin + offset:margin + offset + values.shape[0]]

def dilation(layer_index):
    return POS_DEV * 2 ** layer_index // 4

def reference(inputs, cotangent, conv_kernels, point_weights):
    stream = inputs
    saved = []
    for layer_index in range(LAYERS):
        distance = dilation(layer_index)
        active = jax.nn.gelu(stream.astype(jnp.float32)).astype(jnp.bfloat16)
        taps = [moved(active, (tap_index - 1) * distance) for tap_index in range(3)]
        inner = jnp.dot(taps[0], conv_kernels[layer_index, 0].T, preferred_element_type=jnp.float32)
        for tap_index in (1, 2):
            inner = inner + jnp.dot(taps[tap_index], conv_kernels[layer_index, tap_index].T, preferred_element_type=jnp.float32)
        hidden = jax.nn.gelu(inner).astype(jnp.bfloat16)
        output = stream.astype(jnp.float32) + jnp.dot(hidden, point_weights[layer_index], preferred_element_type=jnp.float32)
        saved.append((stream, taps, inner, hidden))
        stream = output.astype(jnp.bfloat16)
    gradient = cotangent.astype(jnp.float32)
    kernel_list = [None] * LAYERS
    point_list = [None] * LAYERS
    for layer_index in reversed(range(LAYERS)):
        before, taps, inner, hidden = saved[layer_index]
        distance = dilation(layer_index)
        grad_b = gradient.astype(jnp.bfloat16)
        hidden_grad = jnp.dot(grad_b, point_weights[layer_index].T, preferred_element_type=jnp.float32)
        inner_grad = (hidden_grad * gelu_slope(inner)).astype(jnp.bfloat16)
        point_list[layer_index] = jnp.dot(hidden.T, grad_b, preferred_element_type=jnp.float32)
        kernel_list[layer_index] = jnp.stack([jnp.dot(inner_grad.T, taps[tap_index], preferred_element_type=jnp.float32) for tap_index in range(3)])
        back = jnp.dot(moved(inner_grad, distance), conv_kernels[layer_index, 0], preferred_element_type=jnp.float32)
        back = back + jnp.dot(inner_grad, conv_kernels[layer_index, 1], preferred_element_type=jnp.float32)
        back = back + jnp.dot(moved(inner_grad, -distance), conv_kernels[layer_index, 2], preferred_element_type=jnp.float32)
        gradient = gradient + gelu_slope(before.astype(jnp.float32)) * back
    return (gradient, jnp.stack(kernel_list), jnp.stack(point_list))
```

```python
import jax
import jax.numpy as jnp
import numpy as np
from jax import lax
from jax.sharding import PartitionSpec as P

LAYERS = 4
BF16 = jnp.bfloat16
F32 = jnp.float32
ORDER = (0, 3, 1, 2)


def gelu_slope(values):
    return jax.vjp(jax.nn.gelu, values)[1](jnp.ones_like(values))[0]


def dot(a, b, ca, cb):
    return lax.dot_general(a, b, (((ca,), (cb,)), ((), ())), preferred_element_type=F32)


def move(values, axis, by):
    peers = lax.axis_size(axis)
    return lax.ppermute(values, axis, [(i, (i + by) % peers) for i in range(peers)])


def swap(values, axis, mask):
    peers = lax.axis_size(axis)
    return lax.ppermute(values, axis, [(i, i ^ mask) for i in range(peers)])


def gather_channels(shard):
    me = lax.axis_index("mp")
    parts = [shard] + [swap(shard, "mp", mask) for mask in (1, 3, 2)]
    by_mask = {0: parts[0], 1: parts[1], 3: parts[2], 2: parts[3]}
    columns = []
    for owner in range(4):
        mask = me ^ owner
        columns.append(
            jnp.where(
                mask == 0,
                by_mask[0],
                jnp.where(mask == 1, by_mask[1], jnp.where(mask == 2, by_mask[2], by_mask[3])),
            )
        )
    return jnp.concatenate(columns, axis=1)


def shift_both(down, up, distance):
    length = down.shape[0]
    me = lax.axis_index("seq")
    peers = lax.axis_size("seq")
    steps = max(distance // length, 1)
    rows = min(distance, length)
    from_left = move(down[length - rows:], "seq", steps)
    from_right = move(up[:rows], "seq", -steps)
    from_left = jnp.where(me >= steps, from_left, jnp.zeros_like(from_left))
    from_right = jnp.where(me < peers - steps, from_right, jnp.zeros_like(from_right))
    if rows < length:
        from_left = jnp.concatenate([from_left, down[: length - rows]], axis=0)
        from_right = jnp.concatenate([up[rows:], from_right], axis=0)
    return from_left, from_right


def sum_mp(term):
    half = term.shape[1] // 2
    a, b = term[:, :half], term[:, half:]
    a1 = swap(a, "mp", 1)
    b1 = swap(b, "mp", 3)
    a = (a.astype(F32) + a1.astype(F32)).astype(BF16)
    b = (b.astype(F32) + b1.astype(F32)).astype(BF16)
    a2 = swap(a, "mp", 3)
    b2 = swap(b, "mp", 1)
    return jnp.concatenate(
        [a.astype(F32) + a2.astype(F32), b.astype(F32) + b2.astype(F32)], axis=1
    )


def block_masks():
    first = [c + 2 * x + 8 * z for c in (0, 1) for x in ORDER for z in ORDER]
    second = [c + 2 * x + 8 * z for c in (0, 1) for z in ORDER for x in ORDER]
    return np.array(first), np.array(second)


def orderings():
    me = lax.axis_index("seq")
    result = []
    for masks in block_masks():
        column = np.arange(768)
        offset = jnp.asarray(column % 24 // 6 * 192 + column % 6, jnp.int32)
        source = offset + 6 * (me ^ jnp.asarray(masks[column // 24], jnp.int32))
        table = lax.broadcasted_iota(jnp.int32, (768, 768), 0) == source[None]
        table = table.astype(BF16)
        result.append((table[:576], table[576:]))
    return result


def weight_terms(ordering, cat, hidden, active, grad_b):
    right = jnp.concatenate([active, grad_b], axis=0)
    outs = []
    for index, (kernel_order, point_order) in enumerate(ordering):
        left = jnp.concatenate(
            [dot(cat, kernel_order, 1, 0), dot(hidden, point_order, 1, 0)], axis=0
        ).astype(BF16)
        outs.append(dot(left, right[:, index * 768 : (index + 1) * 768], 0, 0).astype(BF16))
    return outs


def halve(values, mask):
    rows = values.shape[0] // 2
    return values[:rows], swap(values[rows:], "seq", mask)


def weight_sum(first, second):
    for step, (m1, m2) in enumerate(((1, 1), (2, 8), (6, 24), (8, 2), (24, 6))):
        a0, a1 = halve(first, m1)
        b0, b1 = halve(second, m2)
        kind = F32 if step == 4 else BF16
        first = (a0.astype(F32) + a1.astype(F32)).astype(kind)
        second = (b0.astype(F32) + b1.astype(F32)).astype(kind)
    return jnp.concatenate([first, second], axis=1)


def shards(inputs, cotangent, conv_kernels, point_weights):
    length = inputs.shape[0]
    me = lax.axis_index("mp")
    stream = gather_channels(inputs)
    gradient = gather_channels(cotangent).astype(F32)
    ordering = orderings()
    kernels = conv_kernels.reshape(LAYERS, 576, 1536)
    saved = []
    for layer in range(LAYERS):
        distance = length * 2**layer // 4
        active = jax.nn.gelu(stream.astype(F32)).astype(BF16)
        taps = dot(active, kernels[layer], 1, 1)
        left, right = shift_both(
            taps[:, :192].astype(BF16), taps[:, 384:].astype(BF16), distance
        )
        inner = taps[:, 192:384] + left.astype(F32) + right.astype(F32)
        hidden = jax.nn.gelu(inner).astype(BF16)
        saved.append((stream, active, inner, hidden))
        if layer < LAYERS - 1:
            term = dot(hidden, point_weights[layer], 1, 0).astype(BF16)
            stream = (stream.astype(F32) + sum_mp(term)).astype(BF16)
    sums = [None] * LAYERS
    for layer in reversed(range(LAYERS)):
        before, active, inner, hidden = saved[layer]
        distance = length * 2**layer // 4
        grad_b = gradient.astype(BF16)
        hidden_grad = dot(grad_b, point_weights[layer], 1, 1)
        inner_grad = (hidden_grad * gelu_slope(inner)).astype(BF16)
        left, right = shift_both(inner_grad, inner_grad, distance)
        cat = jnp.concatenate([right, inner_grad, left], axis=1)
        term = dot(cat, kernels[layer], 1, 0).astype(BF16)
        first, second = weight_terms(ordering, cat, hidden, active, grad_b)
        sums[layer] = weight_sum(first, second)
        if layer > 0:
            gradient = gradient + gelu_slope(before.astype(F32)) * sum_mp(term)
        else:
            own = jnp.zeros(inputs.shape, F32)
            blocks = term.reshape(length, 4, 384).transpose(1, 0, 2)
            total = lax.dynamic_index_in_dim(blocks, me, 0, False).astype(F32)
            for mask in (1, 3, 2):
                sent = lax.dynamic_index_in_dim(blocks, me ^ mask, 0, False)
                total = total + swap(sent, "mp", mask).astype(F32)
            own = lax.dynamic_slice_in_dim(gradient, me * 384, 384, 1)
            gradient = own + gelu_slope(inputs.astype(F32)) * total
    sums = jnp.stack(sums)
    return (gradient, sums[:, :18].reshape(LAYERS, 3, 6, 1536), sums[:, 18:])


def solution(mesh):
    return jax.shard_map(
        shards,
        mesh=mesh,
        in_specs=(P("seq", "mp"), P("seq", "mp"), P(None, None, "mp", None), P(None, "mp", None)),
        out_specs=(
            P("seq", "mp"),
            P(None, None, ("mp", "seq"), None),
            P(None, ("mp", "seq"), None),
        ),
        check_vma=False,
    )
```

```python
import functools

import jax
import jax.numpy as jnp
import numpy as np
from jax import lax
from jax.experimental import pallas as pl
from jax.experimental.pallas import tpu as pltpu
from jax.sharding import PartitionSpec as P

LAYERS = 4
ROWS = 128
C = 1536
H = 192
HALF = C // 2
SHARD = C // 4
PEERS = 32
BF16 = jnp.bfloat16
F32 = jnp.float32
ORDER = (0, 3, 1, 2)
ROOT = float(np.sqrt(2.0 / np.pi))
CUBE = 0.044715


def together(*values):
    return lax.optimization_barrier(values)


def dot(a, b, ca=1, cb=0):
    return lax.dot_general(a, b, (((ca,), (cb,)), ((), ())), preferred_element_type=F32)


def swap(values, axis, mask):
    peers = lax.axis_size(axis)
    return lax.ppermute(values, axis, [(i, i ^ mask) for i in range(peers)])


def add(a, b):
    return (a.astype(F32) + b.astype(F32)).astype(BF16)


def slope(x):
    square = x * x
    t = jnp.tanh(ROOT * x * (1.0 + CUBE * square))
    return 0.5 * (1.0 + t) + 0.5 * x * (1.0 - t * t) * (ROOT * (1.0 + 3.0 * CUBE * square))


def shifted(values, by):
    if by == 0:
        return values
    length = values.shape[0]
    zeros = jnp.zeros((abs(by),) + values.shape[1:], values.dtype)
    if by > 0:
        return jnp.concatenate([values[by:], zeros], axis=0)
    return jnp.concatenate([zeros, values[: length + by]], axis=0)


def struct(shape, kind):
    return jax.ShapeDtypeStruct(shape, kind)


def call(body, outs, scratch, args, spaces=None, flops=4e8):
    spaces = spaces or {}
    return pl.pallas_call(
        body,
        out_shape=outs,
        in_specs=[
            pl.BlockSpec(memory_space=spaces.get(i, pltpu.VMEM)) for i in range(len(args))
        ],
        out_specs=[pl.BlockSpec(memory_space=pltpu.VMEM)] * len(outs),
        scratch_shapes=scratch,
        compiler_params=pltpu.CompilerParams(vmem_limit_bytes=40 * 2**20),
        cost_estimate=pl.CostEstimate(flops=int(flops), bytes_accessed=4_000_000, transcendentals=0),
    )(*args)


WEIGHTS = [
    pltpu.VMEM((3, H, C), BF16),
    pltpu.VMEM((H, C), BF16),
    pltpu.SemaphoreType.DMA,
    pltpu.SemaphoreType.DMA,
]


def fetch(layer, kernels, points, k_mem, p_mem, k_sem, p_sem):
    k_copy = pltpu.make_async_copy(kernels.at[layer], k_mem, k_sem)
    p_copy = pltpu.make_async_copy(points.at[layer], p_mem, p_sem)
    return k_copy, p_copy


def chunks():
    return [slice(i, i + 16) for i in range(0, ROWS, 16)]


def total_of(rows, half, first, second):
    a, b = (first, second)[half]
    return a[rows].astype(F32) + b[rows].astype(F32)


def conv(active, k_mem, distance):
    taps = [dot(active, k_mem[k], 1, 1) for k in range(3)]
    return taps[1] + shifted(taps[0], -distance) + shifted(taps[2], distance)


def conv_back(inner_grad, k_mem, distance):
    out = None
    for k in range(3):
        moved = shifted(inner_grad, (1 - k) * distance).astype(BF16)
        part = dot(moved, k_mem[k])
        out = part if out is None else out + part
    return out


def put_halves(term, ta, tb):
    term = term.astype(BF16)
    ta[...] = term[:, :HALF]
    tb[...] = term[:, HALF:]


def backward_of(inner, grad_b, p_mem):
    hidden_grad = dot(grad_b, p_mem[...], 1, 1)
    return (hidden_grad * slope(inner)).astype(BF16)


def start_kernel(me, own, one, three, two, kernels, points, *rest):
    x, g, active, inner, hidden, ta, tb, k_mem, p_mem, k_sem, p_sem = rest
    k_copy, p_copy = fetch(0, kernels, points, k_mem, p_mem, k_sem, p_sem)
    k_copy.start()
    p_copy.start()
    for mask, block in ((0, own), (1, one), (3, three), (2, two)):
        at = pl.ds(pl.multiple_of((me[0] ^ mask) * SHARD, 128), SHARD)
        x[:, at] = block[:ROWS]
        g[:, at] = block[ROWS:]
    for rows in chunks():
        active[rows] = jax.nn.gelu(x[rows].astype(F32)).astype(BF16)
    k_copy.wait()
    values = conv(active[...], k_mem, 1)
    inner[...] = values
    values = jax.nn.gelu(values).astype(BF16)
    hidden[...] = values
    p_copy.wait()
    put_halves(dot(values, p_mem[...]), ta, tb)


def forward_kernel(layer, x, a, b, a2, b2, kernels, points, *rest):
    x1, active, inner, hidden, ta, tb, k_mem, p_mem, k_sem, p_sem = rest
    k_copy, p_copy = fetch(layer, kernels, points, k_mem, p_mem, k_sem, p_sem)
    k_copy.start()
    p_copy.start()
    advance(x, a, b, a2, b2, x1, active)
    k_copy.wait()
    values = conv(active[...], k_mem, 2**layer)
    inner[...] = values
    values = jax.nn.gelu(values).astype(BF16)
    hidden[...] = values
    p_copy.wait()
    put_halves(dot(values, p_mem[...]), ta, tb)


def advance(x, a, b, a2, b2, x1, active):
    for rows in chunks():
        for half in (0, 1):
            at = slice(half * HALF, half * HALF + HALF)
            total = total_of(rows, half, (a, a2), (b, b2))
            values = (x[rows, at].astype(F32) + total).astype(BF16)
            x1[rows, at] = values
            active[rows, at] = jax.nn.gelu(values.astype(F32)).astype(BF16)


def turn_kernel(layer, x, a, b, a2, b2, g, kernels, points, *rest):
    x1, active, hidden, inner_grad, ta, tb, k_mem, p_mem, k_sem, p_sem = rest
    k_copy, p_copy = fetch(layer, kernels, points, k_mem, p_mem, k_sem, p_sem)
    k_copy.start()
    p_copy.start()
    advance(x, a, b, a2, b2, x1, active)
    k_copy.wait()
    inner = conv(active[...], k_mem, 2**layer)
    hidden[...] = jax.nn.gelu(inner).astype(BF16)
    p_copy.wait()
    values = backward_of(inner, g[...], p_mem)
    inner_grad[...] = values
    put_halves(conv_back(values.astype(F32), k_mem, 2**layer), ta, tb)


def retreat(g, a, b, a2, b2, x, g1, grad_b):
    for rows in chunks():
        for half in (0, 1):
            at = slice(half * HALF, half * HALF + HALF)
            total = total_of(rows, half, (a, a2), (b, b2))
            values = g[rows, at].astype(F32) + slope(x[rows, at].astype(F32)) * total
            if g1 is not None:
                g1[rows, at] = values
            grad_b[rows, at] = values.astype(BF16)


def backward_kernel(layer, g, a, b, a2, b2, x, inner, kernels, points, *rest):
    g1, grad_b, inner_grad, ta, tb, k_mem, p_mem, k_sem, p_sem = rest
    k_copy, p_copy = fetch(layer, kernels, points, k_mem, p_mem, k_sem, p_sem)
    p_copy.start()
    k_copy.start()
    retreat(g, a, b, a2, b2, x, g1, grad_b)
    p_copy.wait()
    values = backward_of(inner[...], grad_b[...], p_mem)
    inner_grad[...] = values
    k_copy.wait()
    put_halves(conv_back(values.astype(F32), k_mem, 2**layer), ta, tb)


def final_kernel(me, g, a, b, a2, b2, x, inner, order, points, *rest):
    grad_b, inner_grad, sent, p_mem, p_sem = rest
    p_copy = pltpu.make_async_copy(points.at[0], p_mem, p_sem)
    p_copy.start()
    retreat(g, a, b, a2, b2, x, None, grad_b)
    p_copy.wait()
    values = backward_of(inner[...], grad_b[...], p_mem)
    inner_grad[...] = values
    own = grad_b[:, pl.ds(pl.multiple_of(me[0] * SHARD, 128), SHARD)]
    parts = jnp.concatenate([values, own[:, :H], own[:, H:]], axis=0)
    sent[...] = dot(order[...], parts).astype(BF16)


def last_kernel(me, got, order, kernels, *rest):
    own, one, three, two, g, k_mem, term, k_sem = rest
    k_copy = pltpu.make_async_copy(kernels.at[0], k_mem, k_sem)
    k_copy.start()
    values = dot(order[...], got[...])
    moved = values.astype(BF16)
    g[:, :H] = values[192:320]
    g[:, H:] = values[320:448]
    k_copy.wait()
    out = dot(moved[64:192], k_mem[0])
    out = out + dot(moved[32:160], k_mem[1])
    term[...] = out + dot(moved[:128], k_mem[2])
    for mask, ref in ((0, own), (1, one), (3, three), (2, two)):
        at = pl.ds(pl.multiple_of((me[0] ^ mask) * SHARD, 128), SHARD)
        ref[...] = term[:, at].astype(ref.dtype)


def weight_kernel(distance, count, inner_grad, hidden, active, grad_b, *rest):
    tables, outs = rest[:count], rest[count:]
    grad = inner_grad[...].astype(F32)
    moved = [shifted(grad, (1 - k) * distance).astype(BF16) for k in range(3)]
    width = C // count
    for index, table in enumerate(tables):
        top = sum(dot(moved[k], table[k * H : (k + 1) * H]) for k in range(3))
        bottom = dot(hidden[...], table[3 * H :])
        left = jnp.concatenate([top, bottom], axis=0).T.astype(BF16)
        at = slice(index * width, (index + 1) * width)
        right = jnp.concatenate([active[:, at], grad_b[:, at]], axis=0)
        for part in (0, 1):
            ref = outs[part * count + index]
            for row in range(0, 384, 128):
                rows = left[part * 384 + row : part * 384 + row + 128]
                ref[row : row + 128] = dot(rows, right).astype(BF16)


def weight_terms(layer, tables, inner_grad, hidden, active, grad_b):
    count = len(tables)
    outs = [struct((384, C // count), BF16)] * (2 * count)
    body = functools.partial(weight_kernel, 2**layer, count)
    return call(body, outs, [], (inner_grad, hidden, active, grad_b, *tables), flops=8e8)


def sums_kernel(first, k0, k1, c0, c1, late, kernel_out, point_out):
    total = first[0].astype(F32)
    for i in range(1, 16):
        total = total + first[i].astype(F32)
    second = [k0[...].astype(F32) + c0[...].astype(F32), k1[...].astype(F32) + c1[...].astype(F32)]
    second = jnp.concatenate(second, axis=1)
    for layer, values in enumerate((total, second, late[0].astype(F32), late[1].astype(F32))):
        for k in range(3):
            kernel_out[layer, k] = values[6 * k : 6 * k + 6]
        point_out[layer] = values[18:]


def table_of(source, columns):
    (source,) = together(jnp.asarray(source, jnp.int32))
    return (lax.broadcasted_iota(jnp.int32, (len(source), columns), 1) == source[:, None]).astype(
        BF16
    )


def by_source(blocks):
    column = np.arange(768)
    row = column % 24
    fixed = jnp.asarray(row // 6 * H + row % 6, jnp.int32)
    (source,) = together(fixed + 6 * jnp.repeat(blocks, 24))
    return (lax.broadcasted_iota(jnp.int32, (768, 768), 0) == source[None]).astype(BF16)


def absolute_order():
    core = lax.axis_index("seq") % 2
    block = np.arange(32)
    return by_source(2 * (block % 16) + (core ^ jnp.asarray(block // 16, jnp.int32)))


def relative_orders():
    me = lax.axis_index("seq")
    first = [c + 2 * x + 8 * z for c in (0, 1) for x in ORDER for z in ORDER]
    second = [c + 2 * x + 8 * z for c in (0, 1) for z in ORDER for x in ORDER]
    return [by_source(me ^ jnp.asarray(masks, jnp.int32)) for masks in (first, second)]


def block_to_residue():
    n = np.arange(256)
    r, t = n // 8, n % 8
    go = t // 4 * 128 + t % 4 * 32 + r
    come = n % 128 // 4 * 8 + n // 128 * 4 + n % 4
    return table_of(go, 256), table_of(come, 256)


def residue_to_block():
    n = np.arange(512)
    s, t = n // 16, n % 16
    a = 4 * s + t - 1
    grad = np.where((t < 6) & (a >= 0) & (a < 128), a, -1)
    half = 128 + (t - 6) // 4 * 128 + 4 * s + (t - 6) % 4
    go = np.where(t < 6, grad, np.where(t < 14, half, -1))
    n = np.arange(448)
    m = n - 192
    come = np.where(
        n < 192, n % 32 * 16 + n // 32, m % 32 * 16 + 6 + m // 128 * 4 + m % 128 // 32
    )
    return table_of(go, 384), table_of(come, 512)


def over_chips(values):
    groups = [[2 * i + core for i in range(PEERS // 2)] for core in (0, 1)]
    return lax.all_to_all(
        values.reshape(16, 24, values.shape[1]), "seq", 0, 0, axis_index_groups=groups
    )


def halving(kept, sent, step):
    masks = ((2, 8), (6, 24), (8, 2), (24, 6))[step]
    return kept, [swap(s, "seq", mask) for s, mask in zip(sent, masks)]


def add_split(kept, come):
    rows = kept[0].shape[0] // 2
    low = [add(k[:rows], c[:rows]) for k, c in zip(kept, come)]
    high = [add(k[rows:], c[rows:]) for k, c in zip(kept, come)]
    return low, high


def over_chips_first(values):
    both = jnp.concatenate([v.reshape(4, 1, 96, C) for v in values], axis=1)
    along_z = [[8 * i + j for i in range(4)] for j in range(8)]
    both = both.reshape(4, len(values) * 96, C)
    return lax.psum_scatter(both, "seq", scatter_dimension=0, axis_index_groups=along_z)


def over_chips_second(part, count):
    along_x = [[8 * z + 2 * i + c for i in range(4)] for z in range(4) for c in range(2)]
    part = part.reshape(count, 4, 24, C).transpose(1, 0, 2, 3).reshape(4, count * 24, C)
    part = lax.psum_scatter(part, "seq", scatter_dimension=0, axis_index_groups=along_x)
    return part.reshape(count, 24, C)


def sum_mp(a, b, first=()):
    a1, b1, *first = together(swap(a, "mp", 1), swap(b, "mp", 3), *first)
    a, b = add(a, a1), add(b, b1)
    a2, b2 = swap(a, "mp", 3), swap(b, "mp", 1)
    kept, sent = first[: len(first) // 2], first[len(first) // 2 :]
    a2, b2, *other = together(a2, b2, *[swap(s, "seq", 1) for s in sent])
    return (a, b, a2, b2), kept, other


def shards(inputs, cotangent, conv_kernels, point_weights):
    me = lax.axis_index("mp").astype(jnp.int32)[None]
    weights = (conv_kernels, point_weights)
    go, come = block_to_residue()
    sent = dot(go, jnp.concatenate([inputs, cotangent], axis=0)).astype(BF16)
    got = lax.all_to_all(sent.reshape(PEERS, 8, SHARD), "seq", 0, 0)
    own = dot(come, got.reshape(256, SHARD)).astype(BF16)
    one, three, two = (swap(own, "mp", mask) for mask in (1, 3, 2))
    full, inner_like, hid = struct((ROWS, C), BF16), struct((ROWS, H), F32), struct((ROWS, H), BF16)
    half = struct((ROWS, HALF), BF16)
    x, g, active, inner, hidden, ta, tb = call(
        start_kernel,
        [full, full, full, inner_like, hid, half, half],
        WEIGHTS,
        (me, own, one, three, two, *weights),
        {0: pltpu.SMEM, 5: pl.ANY, 6: pl.ANY},
    )
    saved = [(x, active, inner, hidden)]
    table = absolute_order()
    relative = relative_orders()
    block_go, block_come = residue_to_block()
    for layer in (1, 2):
        terms, _, _ = sum_mp(ta, tb)
        x, active, inner, hidden, ta, tb = call(
            functools.partial(forward_kernel, layer),
            [full, full, inner_like, hid, half, half],
            WEIGHTS,
            (x, *terms, *weights),
            {5: pl.ANY, 6: pl.ANY},
        )
        saved.append((x, active, inner, hidden))
    terms, _, _ = sum_mp(ta, tb)
    x, active, hidden, inner_grad, ta, tb = call(
        functools.partial(turn_kernel, 3),
        [full, full, hid, hid, half, half],
        WEIGHTS,
        (x, *terms, g, *weights),
        {6: pl.ANY, 7: pl.ANY},
    )
    grad_b = g
    halves = [None] * LAYERS
    for layer in (3, 2, 1):
        tables = [table] if layer > 1 else relative
        first = weight_terms(layer, tables, inner_grad, hidden, active, grad_b)
        terms, kept, other = sum_mp(ta, tb, first)
        halves[layer] = (kept, other)
        above, (x, active, inner, hidden) = x, saved[layer - 1]
        if layer > 1:
            g, grad_b, inner_grad, ta, tb = call(
                functools.partial(backward_kernel, layer - 1),
                [struct((ROWS, C), F32), full, hid, half, half],
                WEIGHTS,
                (g, *terms, above, inner, *weights),
                {7: pl.ANY, 8: pl.ANY},
            )
    late = over_chips_first([add(halves[n][0][0], halves[n][1][0]) for n in (2, 3)])
    kept, sent = add_split(*halves[1])
    grad_b, inner_grad, sent_blocks = call(
        final_kernel,
        [full, hid, struct((512, H), BF16)],
        [pltpu.VMEM((H, C), BF16), pltpu.SemaphoreType.DMA],
        (me, g, *terms, above, inner, block_go, point_weights),
        {0: pltpu.SMEM, 9: pl.ANY},
    )
    got = lax.all_to_all(sent_blocks.reshape(PEERS, 16, H), "seq", 0, 0)
    keep, send = weight_terms(0, [table], inner_grad, hidden, active, grad_b)
    other = swap(send, "seq", 1)
    kept, moved = halving(kept, sent, 0)
    got, other, late, *moved = together(got, other, late, *moved)
    kept, sent = add_split(kept, moved)
    late = over_chips_second(late, 2)
    first = over_chips(add(keep, other))
    piece = struct((ROWS, SHARD), BF16)
    total, one, three, two, gradient = call(
        last_kernel,
        [struct((ROWS, SHARD), F32), piece, piece, piece, struct((ROWS, SHARD), F32)],
        [pltpu.VMEM((3, H, C), BF16), pltpu.VMEM((ROWS, C), F32), pltpu.SemaphoreType.DMA],
        (me, got.reshape(512, H), block_come, conv_kernels),
        {0: pltpu.SMEM, 3: pl.ANY},
    )
    got = [swap(s, "mp", mask) for s, mask in ((one, 1), (three, 3), (two, 2))]
    kept, moved = halving(kept, sent, 1)
    *got, move0, move1 = together(*got, *moved)
    for g in got:
        total = total + g.astype(F32)
    gradient = gradient + slope(inputs.astype(F32)) * total
    kept, sent = add_split(kept, (move0, move1))
    kept, moved = halving(kept, sent, 2)
    kept, sent = add_split(kept, moved)
    kept, moved = halving(kept, sent, 3)
    kernel_grad, point_grad = call(
        sums_kernel,
        [struct((LAYERS, 3, 6, C), F32), struct((LAYERS, 6, C), F32)],
        [],
        (first, *kept, *moved, late),
    )
    return gradient, kernel_grad, point_grad


def solution(mesh):
    return jax.shard_map(
        shards,
        mesh=mesh,
        in_specs=(P("seq", "mp"), P("seq", "mp"), P(None, None, "mp", None), P(None, "mp", None)),
        out_specs=(
            P("seq", "mp"),
            P(None, None, ("mp", "seq"), None),
            P(None, ("mp", "seq"), None),
        ),
        check_vma=False,
    )
```

```python
import functools

import jax
import jax.numpy as jnp
import numpy as np
from jax import lax
from jax.experimental import pallas as pl
from jax.experimental.pallas import tpu as pltpu
from jax.sharding import PartitionSpec as P

LAYERS = 4
ROWS = 128
C = 1536
H = 192
HALF = C // 2
SHARD = C // 4
PEERS = 32
BF16 = jnp.bfloat16
F32 = jnp.float32
ROOT = float(np.sqrt(2.0 / np.pi))
CUBE = 0.044715


def together(*values):
    return lax.optimization_barrier(values)


def dot(a, b, ca=1, cb=0):
    return lax.dot_general(a, b, (((ca,), (cb,)), ((), ())), preferred_element_type=F32)


def swap(values, axis, mask):
    peers = lax.axis_size(axis)
    return lax.ppermute(values, axis, [(i, i ^ mask) for i in range(peers)])


def add(a, b):
    return (a.astype(F32) + b.astype(F32)).astype(BF16)


def slope(x):
    square = x * x
    t = jnp.tanh(ROOT * x * (1.0 + CUBE * square))
    return 0.5 * (1.0 + t) + 0.5 * x * (1.0 - t * t) * (ROOT * (1.0 + 3.0 * CUBE * square))


def shifted(values, by):
    if by == 0:
        return values
    length = values.shape[0]
    zeros = jnp.zeros((abs(by),) + values.shape[1:], values.dtype)
    if by > 0:
        return jnp.concatenate([values[by:], zeros], axis=0)
    return jnp.concatenate([zeros, values[: length + by]], axis=0)


def struct(shape, kind):
    return jax.ShapeDtypeStruct(shape, kind)


def call(body, outs, scratch, args, spaces=None, flops=4e8):
    spaces = spaces or {}
    return pl.pallas_call(
        body,
        out_shape=outs,
        in_specs=[
            pl.BlockSpec(memory_space=spaces.get(i, pltpu.VMEM)) for i in range(len(args))
        ],
        out_specs=[pl.BlockSpec(memory_space=pltpu.VMEM)] * len(outs),
        scratch_shapes=scratch,
        compiler_params=pltpu.CompilerParams(vmem_limit_bytes=16 * 2**20),
        cost_estimate=pl.CostEstimate(flops=int(flops), bytes_accessed=4_000_000, transcendentals=0),
    )(*args)


def chunks():
    return [slice(i, i + 16) for i in range(0, ROWS, 16)]


def total_of(rows, half, first, second):
    a, b = (first, second)[half]
    return a[rows].astype(F32) + b[rows].astype(F32)


def conv(active, k_mem, distance):
    taps = [dot(active, k_mem[k], 1, 1) for k in range(3)]
    return taps[1] + shifted(taps[0], -distance) + shifted(taps[2], distance)


def conv_back(inner_grad, k_mem, distance):
    out = None
    for k in range(3):
        moved = shifted(inner_grad, (1 - k) * distance).astype(BF16)
        part = dot(moved, k_mem[k])
        out = part if out is None else out + part
    return out


def put_halves(term, ta, tb):
    term = term.astype(BF16)
    ta[...] = term[:, :HALF]
    tb[...] = term[:, HALF:]


def backward_of(inner, grad_b, p_mem):
    hidden_grad = dot(grad_b, p_mem[...], 1, 1)
    return (hidden_grad * slope(inner)).astype(BF16)


def start_kernel(me, own, one, three, two, k_mem, p_mem, *rest):
    x, g, inner, ta, tb, active = rest
    for mask, block in ((0, own), (1, one), (3, three), (2, two)):
        at = pl.ds(pl.multiple_of((me[0] ^ mask) * SHARD, 128), SHARD)
        x[:, at] = block[:ROWS]
        g[:, at] = block[ROWS:]
    for rows in chunks():
        active[rows] = jax.nn.gelu(x[rows].astype(F32)).astype(BF16)
    values = conv(active[...], k_mem, 1)
    inner[...] = values
    put_halves(dot(jax.nn.gelu(values).astype(BF16), p_mem[...]), ta, tb)


def forward_kernel(layer, x, a, b, a2, b2, k_mem, p_mem, *rest):
    x1, inner, ta, tb, active = rest
    advance(x, a, b, a2, b2, x1, active)
    values = conv(active[...], k_mem, 2**layer)
    inner[...] = values
    put_halves(dot(jax.nn.gelu(values).astype(BF16), p_mem[...]), ta, tb)


def advance(x, a, b, a2, b2, x1, active):
    for rows in chunks():
        for half in (0, 1):
            at = slice(half * HALF, half * HALF + HALF)
            total = total_of(rows, half, (a, a2), (b, b2))
            values = (x[rows, at].astype(F32) + total).astype(BF16)
            x1[rows, at] = values
            active[rows, at] = jax.nn.gelu(values.astype(F32)).astype(BF16)


def turn_kernel(layer, x, a, b, a2, b2, g, k_mem, p_mem, *rest):
    x1, inner, inner_grad, ta, tb, active = rest
    advance(x, a, b, a2, b2, x1, active)
    before = conv(active[...], k_mem, 2**layer)
    inner[...] = before
    values = backward_of(before, g[...], p_mem)
    inner_grad[...] = values
    put_halves(conv_back(values.astype(F32), k_mem, 2**layer), ta, tb)


def retreat(g, a, b, a2, b2, x, g1, grad_b):
    for rows in chunks():
        for half in (0, 1):
            at = slice(half * HALF, half * HALF + HALF)
            total = total_of(rows, half, (a, a2), (b, b2))
            values = g[rows, at].astype(F32) + slope(x[rows, at].astype(F32)) * total
            if g1 is not None:
                g1[rows, at] = values
            grad_b[rows, at] = values.astype(BF16)


def backward_kernel(layer, g, a, b, a2, b2, x, inner, k_mem, p_mem, *rest):
    g1, grad_b, inner_grad, ta, tb = rest
    retreat(g, a, b, a2, b2, x, g1, grad_b)
    values = backward_of(inner[...], grad_b[...], p_mem)
    inner_grad[...] = values
    put_halves(conv_back(values.astype(F32), k_mem, 2**layer), ta, tb)


def final_kernel(me, g, a, b, a2, b2, x, inner, order, p_mem, *rest):
    grad_b, inner_grad, sent = rest
    retreat(g, a, b, a2, b2, x, None, grad_b)
    values = backward_of(inner[...], grad_b[...], p_mem)
    inner_grad[...] = values
    own = grad_b[:, pl.ds(pl.multiple_of(me[0] * SHARD, 128), SHARD)]
    parts = jnp.concatenate([values, own[:, :H], own[:, H:]], axis=0)
    sent[...] = dot(order[...], parts).astype(BF16)


def last_kernel(me, got, order, k_mem, *rest):
    own, one, three, two, g, term = rest
    values = dot(order[...], got[...])
    moved = values.astype(BF16)
    g[:, :H] = values[192:320]
    g[:, H:] = values[320:448]
    out = dot(moved[64:192], k_mem[0])
    out = out + dot(moved[32:160], k_mem[1])
    term[...] = out + dot(moved[:128], k_mem[2])
    for mask, ref in ((0, own), (1, one), (3, three), (2, two)):
        at = pl.ds(pl.multiple_of((me[0] ^ mask) * SHARD, 128), SHARD)
        ref[...] = term[:, at].astype(ref.dtype)


def weight_kernel(distance, inner_grad, inner, x, grad_b, table, keep, send):
    grad = inner_grad[...].astype(F32)
    top = None
    for k in range(3):
        moved = shifted(grad, (1 - k) * distance).astype(BF16)
        part = dot(moved, table[k * H : (k + 1) * H])
        top = part if top is None else top + part
    bottom = dot(jax.nn.gelu(inner[...]).astype(BF16), table[3 * H :])
    left = jnp.concatenate([top, bottom], axis=0).T.astype(BF16)
    for column in range(0, C, 384):
        at = slice(column, column + 384)
        active = jax.nn.gelu(x[:, at].astype(F32)).astype(BF16)
        right = jnp.concatenate([active, grad_b[:, at]], axis=0)
        for ref, row in ((keep, 0), (send, 384)):
            ref[:, at] = dot(left[row : row + 384], right).astype(BF16)


def weight_terms(layer, table, inner_grad, inner, x, grad_b):
    body = functools.partial(weight_kernel, 2**layer)
    outs = [struct((384, C), BF16)] * 2
    return call(body, outs, [], (inner_grad, inner, x, grad_b, table), flops=8e8)


def merge_kernel(*refs):
    out = refs[-1]
    for layer in range(len(refs) // 2):
        a, b = refs[2 * layer], refs[2 * layer + 1]
        for z in range(4):
            rows = slice(96 * z, 96 * z + 96)
            out[z, 96 * layer : 96 * layer + 96] = add(a[rows], b[rows])


def split_kernel(me, *refs):
    parts, outs = refs[:-4], refs[-4:]
    for mask, out in enumerate(outs):
        at = me[0] ^ mask
        row = 0
        for part in parts:
            for layer in range(part.shape[0] // 96):
                rows = pl.ds(pl.multiple_of(96 * layer + 24 * at, 8), 24)
                out[row : row + 24] = part[rows]
                row += 24


def sums_kernel(first, own, one, two, three, kernel_out, point_out):
    total = first[0].astype(F32)
    for i in range(1, 16):
        total = total + first[i].astype(F32)
    late = own[...].astype(F32)
    for ref in (one, two, three):
        late = late + ref[...].astype(F32)
    for layer, values in enumerate((total, late[24:48], late[48:], late[:24])):
        for k in range(3):
            kernel_out[layer, k] = values[6 * k : 6 * k + 6]
        point_out[layer] = values[18:]


def table_of(source, columns):
    (source,) = together(jnp.asarray(source, jnp.int32))
    return (lax.broadcasted_iota(jnp.int32, (len(source), columns), 1) == source[:, None]).astype(
        BF16
    )


def by_source(blocks):
    column = np.arange(768)
    row = column % 24
    fixed = jnp.asarray(row // 6 * H + row % 6, jnp.int32)
    (source,) = together(fixed + 6 * jnp.repeat(blocks, 24))
    return (lax.broadcasted_iota(jnp.int32, (768, 768), 0) == source[None]).astype(BF16)


def absolute_order():
    core = lax.axis_index("seq") % 2
    block = np.arange(32)
    return by_source(2 * (block % 16) + (core ^ jnp.asarray(block // 16, jnp.int32)))


def block_to_residue():
    n = np.arange(256)
    r, t = n // 8, n % 8
    go = t // 4 * 128 + t % 4 * 32 + r
    come = n % 128 // 4 * 8 + n // 128 * 4 + n % 4
    return table_of(go, 256), table_of(come, 256)


def residue_to_block():
    n = np.arange(512)
    s, t = n // 16, n % 16
    a = 4 * s + t - 1
    grad = np.where((t < 6) & (a >= 0) & (a < 128), a, -1)
    half = 128 + (t - 6) // 4 * 128 + 4 * s + (t - 6) % 4
    go = np.where(t < 6, grad, np.where(t < 14, half, -1))
    n = np.arange(448)
    m = n - 192
    come = np.where(
        n < 192, n % 32 * 16 + n // 32, m % 32 * 16 + 6 + m // 128 * 4 + m % 128 // 32
    )
    return table_of(go, 384), table_of(come, 512)


def over_chips(values):
    groups = [[2 * i + core for i in range(PEERS // 2)] for core in (0, 1)]
    return lax.all_to_all(
        values.reshape(16, 24, values.shape[1]), "seq", 0, 0, axis_index_groups=groups
    )


def over_z(values):
    along_z = [[8 * i + j for i in range(4)] for j in range(8)]
    got = lax.psum_scatter(values, "seq", scatter_dimension=0, axis_index_groups=along_z)
    return got


def sum_mp(a, b, load, first=()):
    a1, b1, *first = together(swap(a, "mp", 1), swap(b, "mp", 3), *first)
    a, b = add(a, a1), add(b, b1)
    a2, b2 = swap(a, "mp", 3), swap(b, "mp", 1)
    sent = [swap(s, "seq", 1) for s in first[1:]]
    loaded = load(a)
    a2, b2, *rest = together(a2, b2, *sent, *loaded)
    kept = [*first[:1], *rest[: len(sent)]]
    return (a, b, a2, b2), kept, rest[len(sent) :]


def shards(inputs, cotangent, conv_kernels, point_weights):
    me = lax.axis_index("mp").astype(jnp.int32)[None]
    along_x = (lax.axis_index("seq") // 2 % 4).astype(jnp.int32)[None]

    def weights(layer):
        def load(after):
            _, kernels, points = together(after, conv_kernels, point_weights)
            return kernels[layer], points[layer]

        return load

    go, come = block_to_residue()
    sent = dot(go, jnp.concatenate([inputs, cotangent], axis=0)).astype(BF16)
    got = lax.all_to_all(sent.reshape(PEERS, 8, SHARD), "seq", 0, 0)
    own = dot(come, got.reshape(256, SHARD)).astype(BF16)
    loaded = weights(0)(own)
    one, three, two, *loaded = together(*[swap(own, "mp", mask) for mask in (1, 3, 2)], *loaded)
    full, narrow, hid = struct((ROWS, C), BF16), struct((ROWS, H), F32), struct((ROWS, H), BF16)
    half = struct((ROWS, HALF), BF16)
    scratch = [pltpu.VMEM((ROWS, C), BF16)]
    x, g, inner, ta, tb = call(
        start_kernel,
        [full, full, narrow, half, half],
        scratch,
        (me, own, one, three, two, *loaded),
        {0: pltpu.SMEM},
    )
    saved = [(x, inner)]
    table = absolute_order()
    block_go, block_come = residue_to_block()
    for layer in (1, 2):
        terms, _, loaded = sum_mp(ta, tb, weights(layer))
        x, inner, ta, tb = call(
            functools.partial(forward_kernel, layer),
            [full, narrow, half, half],
            scratch,
            (x, *terms, *loaded),
        )
        saved.append((x, inner))
    terms, _, loaded = sum_mp(ta, tb, weights(3))
    x, inner, inner_grad, ta, tb = call(
        functools.partial(turn_kernel, 3),
        [full, narrow, hid, half, half],
        scratch,
        (x, *terms, g, *loaded),
    )
    grad_b = g
    halves = [None] * LAYERS
    for layer in (3, 2, 1):
        first = weight_terms(layer, table, inner_grad, inner, x, grad_b)
        terms, halves[layer], loaded = sum_mp(ta, tb, weights(layer - 1), first)
        above, (x, inner) = x, saved[layer - 1]
        if layer == 3:
            (merged,) = call(merge_kernel, [struct((4, 96, C), BF16)], [], halves[3])
            late = over_z(merged)
        if layer > 1:
            g, grad_b, inner_grad, ta, tb = call(
                functools.partial(backward_kernel, layer - 1),
                [struct((ROWS, C), F32), full, hid, half, half],
                [],
                (g, *terms, above, inner, *loaded),
            )
    (merged,) = call(merge_kernel, [struct((4, 192, C), BF16)], [], halves[1] + halves[2])
    later = over_z(merged)
    grad_b, inner_grad, sent_blocks = call(
        final_kernel,
        [full, hid, struct((512, H), BF16)],
        [],
        (me, g, *terms, above, inner, block_go, loaded[1]),
        {0: pltpu.SMEM},
    )
    got = lax.all_to_all(sent_blocks.reshape(PEERS, 16, H), "seq", 0, 0)
    keep, send = weight_terms(0, table, inner_grad, inner, x, grad_b)
    other = swap(send, "seq", 1)
    got, other = together(got, other)
    first = over_chips(add(keep, other))
    piece = struct((ROWS, SHARD), BF16)
    total, one, three, two, gradient = call(
        last_kernel,
        [struct((ROWS, SHARD), F32), piece, piece, piece, struct((ROWS, SHARD), F32)],
        [pltpu.VMEM((ROWS, C), F32)],
        (me, got.reshape(512, H), block_come, loaded[0]),
        {0: pltpu.SMEM},
    )
    for s, mask in ((one, 1), (three, 3), (two, 2)):
        total = total + swap(s, "mp", mask).astype(F32)
    gradient = gradient + slope(inputs.astype(F32)) * total
    own, *sent = call(
        split_kernel,
        [struct((72, C), BF16)] * 4,
        [],
        (along_x, late.reshape(96, C), later.reshape(192, C)),
        {0: pltpu.SMEM},
    )
    parts = [swap(s, "seq", 2 * mask) for mask, s in zip((1, 2, 3), sent)]
    kernel_grad, point_grad = call(
        sums_kernel,
        [struct((LAYERS, 3, 6, C), F32), struct((LAYERS, 6, C), F32)],
        [],
        (first, own, *parts),
    )
    return gradient, kernel_grad, point_grad


def solution(mesh):
    return jax.shard_map(
        shards,
        mesh=mesh,
        in_specs=(P("seq", "mp"), P("seq", "mp"), P(None, None, "mp", None), P(None, "mp", None)),
        out_specs=(
            P("seq", "mp"),
            P(None, None, ("mp", "seq"), None),
            P(None, ("mp", "seq"), None),
        ),
        check_vma=False,
    )
```

```python
import functools

import jax
import jax.numpy as jnp
import numpy as np
from jax import lax
from jax.experimental import pallas as pl
from jax.experimental.pallas import tpu as pltpu
from jax.sharding import PartitionSpec as P

LAYERS = 4
ROWS = 128
C = 1536
H = 192
HALF = C // 2
SHARD = C // 4
PEERS = 32
BF16 = jnp.bfloat16
F32 = jnp.float32
ORDER = (0, 3, 1, 2)
X, Z = 2, 8
ROOT = float(np.sqrt(2.0 / np.pi))
CUBE = 0.044715


def together(*values):
    return lax.optimization_barrier(values)


def dot(a, b, ca=1, cb=0):
    return lax.dot_general(a, b, (((ca,), (cb,)), ((), ())), preferred_element_type=F32)


def swap(values, axis, mask):
    peers = lax.axis_size(axis)
    return lax.ppermute(values, axis, [(i, i ^ mask) for i in range(peers)])


def add(a, b):
    return (a.astype(F32) + b.astype(F32)).astype(BF16)


def slope(x):
    square = x * x
    t = jnp.tanh(ROOT * x * (1.0 + CUBE * square))
    return 0.5 * (1.0 + t) + 0.5 * x * (1.0 - t * t) * (ROOT * (1.0 + 3.0 * CUBE * square))


def shifted(values, by):
    if by == 0:
        return values
    length = values.shape[0]
    zeros = jnp.zeros((abs(by),) + values.shape[1:], values.dtype)
    if by > 0:
        return jnp.concatenate([values[by:], zeros], axis=0)
    return jnp.concatenate([zeros, values[: length + by]], axis=0)


def struct(shape, kind):
    return jax.ShapeDtypeStruct(shape, kind)


def call(body, outs, scratch, args, spaces=None, flops=4e8):
    spaces = spaces or {}
    return pl.pallas_call(
        body,
        out_shape=outs,
        in_specs=[
            pl.BlockSpec(memory_space=spaces.get(i, pltpu.VMEM)) for i in range(len(args))
        ],
        out_specs=[pl.BlockSpec(memory_space=pltpu.VMEM)] * len(outs),
        scratch_shapes=scratch,
        compiler_params=pltpu.CompilerParams(vmem_limit_bytes=16 * 2**20),
        cost_estimate=pl.CostEstimate(flops=int(flops), bytes_accessed=4_000_000, transcendentals=0),
    )(*args)


def chunks():
    return [slice(i, i + 16) for i in range(0, ROWS, 16)]


def total_of(rows, half, first, second):
    a, b = (first, second)[half]
    return a[rows].astype(F32) + b[rows].astype(F32)


def conv(active, k_mem, distance):
    taps = [dot(active, k_mem[k], 1, 1) for k in range(3)]
    return taps[1] + shifted(taps[0], -distance) + shifted(taps[2], distance)


def conv_back(inner_grad, k_mem, distance):
    out = None
    for k in range(3):
        moved = shifted(inner_grad, (1 - k) * distance).astype(BF16)
        part = dot(moved, k_mem[k])
        out = part if out is None else out + part
    return out


def put_halves(term, ta, tb):
    term = term.astype(BF16)
    ta[...] = term[:, :HALF]
    tb[...] = term[:, HALF:]


def backward_of(inner, grad_b, p_mem):
    hidden_grad = dot(grad_b, p_mem[...], 1, 1)
    return (hidden_grad * slope(inner)).astype(BF16)


def start_kernel(me, own, one, three, two, k_mem, p_mem, *rest):
    x, g, inner, ta, tb, active = rest
    for mask, block in ((0, own), (1, one), (3, three), (2, two)):
        at = pl.ds(pl.multiple_of((me[0] ^ mask) * SHARD, 128), SHARD)
        x[:, at] = block[:ROWS]
        g[:, at] = block[ROWS:]
    for rows in chunks():
        active[rows] = jax.nn.gelu(x[rows].astype(F32)).astype(BF16)
    values = conv(active[...], k_mem, 1)
    inner[...] = values
    put_halves(dot(jax.nn.gelu(values).astype(BF16), p_mem[...]), ta, tb)


def forward_kernel(layer, x, a, b, a2, b2, k_mem, p_mem, *rest):
    x1, inner, ta, tb, active = rest
    advance(x, a, b, a2, b2, x1, active)
    values = conv(active[...], k_mem, 2**layer)
    inner[...] = values
    put_halves(dot(jax.nn.gelu(values).astype(BF16), p_mem[...]), ta, tb)


def advance(x, a, b, a2, b2, x1, active):
    for rows in chunks():
        for half in (0, 1):
            at = slice(half * HALF, half * HALF + HALF)
            total = total_of(rows, half, (a, a2), (b, b2))
            values = (x[rows, at].astype(F32) + total).astype(BF16)
            x1[rows, at] = values
            active[rows, at] = jax.nn.gelu(values.astype(F32)).astype(BF16)


def turn_kernel(layer, x, a, b, a2, b2, g, k_mem, p_mem, *rest):
    x1, inner, inner_grad, ta, tb, active = rest
    advance(x, a, b, a2, b2, x1, active)
    before = conv(active[...], k_mem, 2**layer)
    inner[...] = before
    values = backward_of(before, g[...], p_mem)
    inner_grad[...] = values
    put_halves(conv_back(values.astype(F32), k_mem, 2**layer), ta, tb)


def retreat(g, a, b, a2, b2, x, g1, grad_b):
    for rows in chunks():
        for half in (0, 1):
            at = slice(half * HALF, half * HALF + HALF)
            total = total_of(rows, half, (a, a2), (b, b2))
            values = g[rows, at].astype(F32) + slope(x[rows, at].astype(F32)) * total
            if g1 is not None:
                g1[rows, at] = values
            grad_b[rows, at] = values.astype(BF16)


def backward_kernel(layer, g, a, b, a2, b2, x, inner, k_mem, p_mem, *rest):
    g1, grad_b, inner_grad, ta, tb = rest
    retreat(g, a, b, a2, b2, x, g1, grad_b)
    values = backward_of(inner[...], grad_b[...], p_mem)
    inner_grad[...] = values
    put_halves(conv_back(values.astype(F32), k_mem, 2**layer), ta, tb)


def final_kernel(me, g, a, b, a2, b2, x, inner, order, p_mem, *rest):
    grad_b, inner_grad, sent = rest
    retreat(g, a, b, a2, b2, x, None, grad_b)
    values = backward_of(inner[...], grad_b[...], p_mem)
    inner_grad[...] = values
    own = grad_b[:, pl.ds(pl.multiple_of(me[0] * SHARD, 128), SHARD)]
    parts = jnp.concatenate([values, own[:, :H], own[:, H:]], axis=0)
    sent[...] = dot(order[...], parts).astype(BF16)


def last_kernel(me, got, order, k_mem, *rest):
    own, one, three, two, g, term = rest
    values = dot(order[...], got[...])
    moved = values.astype(BF16)
    g[:, :H] = values[192:320]
    g[:, H:] = values[320:448]
    out = dot(moved[64:192], k_mem[0])
    out = out + dot(moved[32:160], k_mem[1])
    term[...] = out + dot(moved[:128], k_mem[2])
    for mask, ref in ((0, own), (1, one), (3, three), (2, two)):
        at = pl.ds(pl.multiple_of((me[0] ^ mask) * SHARD, 128), SHARD)
        ref[...] = term[:, at].astype(ref.dtype)


def weight_kernel(distance, inner_grad, inner, x, grad_b, table, keep, send):
    grad = inner_grad[...].astype(F32)
    top = None
    for k in range(3):
        moved = shifted(grad, (1 - k) * distance).astype(BF16)
        part = dot(moved, table[k * H : (k + 1) * H])
        top = part if top is None else top + part
    bottom = dot(jax.nn.gelu(inner[...]).astype(BF16), table[3 * H :])
    left = jnp.concatenate([top, bottom], axis=0).T.astype(BF16)
    for column in range(0, C, 384):
        at = slice(column, column + 384)
        active = jax.nn.gelu(x[:, at].astype(F32)).astype(BF16)
        right = jnp.concatenate([active, grad_b[:, at]], axis=0)
        for ref, row in ((keep, 0), (send, 384)):
            ref[:, at] = dot(left[row : row + 384], right).astype(BF16)


def weight_terms(layer, table, inner_grad, inner, x, grad_b):
    body = functools.partial(weight_kernel, 2**layer)
    outs = [struct((384, C), BF16)] * 2
    return call(body, outs, [], (inner_grad, inner, x, grad_b, table), flops=8e8)


def merge_kernel(kept, other, *outs):
    size = outs[0].shape[0]
    for number, out in enumerate(outs):
        rows = slice(size * number, size * number + size)
        out[...] = add(kept[rows], other[rows])


def merge(kept, other, count):
    return call(
        merge_kernel, [struct((384 // count, C), BF16)] * count, [], (kept, other), flops=1e7
    )


def sums_kernel(first, kept, come, late_kept, late_come, kernel_out, point_out):
    total = first[0].astype(F32)
    for i in range(1, 16):
        total = total + first[i].astype(F32)
    second = kept[...].astype(F32) + come[...].astype(F32)
    late = late_kept[...].astype(F32) + late_come[...].astype(F32)
    layers = (total, second, late[:24], late[24:])
    for row in range(24):
        values = jnp.concatenate([v[row : row + 1] for v in layers], axis=0)
        if row < 18:
            kernel_out[row // 6, row % 6] = values
        else:
            point_out[row - 18] = values


def table_of(source, columns):
    (source,) = together(jnp.asarray(source, jnp.int32))
    return (lax.broadcasted_iota(jnp.int32, (len(source), columns), 1) == source[:, None]).astype(
        BF16
    )


def by_source(blocks):
    column = np.arange(768)
    row = column % 24
    (source,) = together(jnp.asarray(row // 6 * H + row % 6, jnp.int32) + 6 * blocks)
    return (lax.broadcasted_iota(jnp.int32, (768, 768), 0) == source[None]).astype(BF16)


def absolute_order():
    core = lax.axis_index("seq") % 2
    block = np.arange(768) // 24
    return by_source(
        jnp.asarray(2 * (block % 16), jnp.int32) + (core ^ jnp.asarray(block // 16, jnp.int32))
    )


def relative_order(outer, inner):
    me = lax.axis_index("seq")
    masks = [c + outer * i + inner * j for c in (0, 1) for i in ORDER for j in ORDER]
    return by_source(me ^ jnp.asarray(np.repeat(masks, 24), jnp.int32))


def block_to_residue():
    n = np.arange(256)
    r, t = n // 8, n % 8
    go = t // 4 * 128 + t % 4 * 32 + r
    come = n % 128 // 4 * 8 + n // 128 * 4 + n % 4
    return table_of(go, 256), table_of(come, 256)


def residue_to_block():
    n = np.arange(512)
    s, t = n // 16, n % 16
    a = 4 * s + t - 1
    grad = np.where((t < 6) & (a >= 0) & (a < 128), a, -1)
    half = 128 + (t - 6) // 4 * 128 + 4 * s + (t - 6) % 4
    go = np.where(t < 6, grad, np.where(t < 14, half, -1))
    n = np.arange(448)
    m = n - 192
    come = np.where(
        n < 192, n % 32 * 16 + n // 32, m % 32 * 16 + 6 + m // 128 * 4 + m % 128 // 32
    )
    return table_of(go, 384), table_of(come, 512)


def halved(kept, come):
    rows = kept.shape[0] // 2
    return add(kept[:rows], come[:rows]), add(kept[rows:], come[rows:])


def over_chips(values):
    groups = [[2 * i + core for i in range(PEERS // 2)] for core in (0, 1)]
    return lax.all_to_all(
        values.reshape(16, 24, values.shape[1]), "seq", 0, 0, axis_index_groups=groups
    )


def sum_mp(a, b, load, first=(), second=()):
    a1, b1, *first = together(swap(a, "mp", 1), swap(b, "mp", 3), *first)
    a, b = add(a, a1), add(b, b1)
    loaded = load(a)
    a2, b2, *rest = together(swap(a, "mp", 3), swap(b, "mp", 1), *second, *loaded)
    return (a, b, a2, b2), rest[len(second) :], first, rest[: len(second)]


def shards(inputs, cotangent, conv_kernels, point_weights):
    me = lax.axis_index("mp").astype(jnp.int32)[None]

    def weights(layer):
        def load(after):
            _, kernels, points = together(after, conv_kernels, point_weights)
            return kernels[layer], points[layer]

        return load

    go, come = block_to_residue()
    sent = dot(go, jnp.concatenate([inputs, cotangent], axis=0)).astype(BF16)
    got = lax.all_to_all(sent.reshape(PEERS, 8, SHARD), "seq", 0, 0)
    own = dot(come, got.reshape(256, SHARD)).astype(BF16)
    loaded = weights(0)(own)
    one, three, two, *loaded = together(*[swap(own, "mp", mask) for mask in (1, 3, 2)], *loaded)
    full, narrow, hid = struct((ROWS, C), BF16), struct((ROWS, H), F32), struct((ROWS, H), BF16)
    half = struct((ROWS, HALF), BF16)
    scratch = [pltpu.VMEM((ROWS, C), BF16)]
    x, g, inner, ta, tb = call(
        start_kernel,
        [full, full, narrow, half, half],
        scratch,
        (me, own, one, three, two, *loaded),
        {0: pltpu.SMEM},
    )
    saved = [(x, inner)]
    tables = {2: relative_order(Z, X), 1: relative_order(X, Z), 0: absolute_order()}
    tables[3] = tables[2]
    block_go, block_come = residue_to_block()
    for layer in (1, 2):
        terms, loaded, _, _ = sum_mp(ta, tb, weights(layer))
        x, inner, ta, tb = call(
            functools.partial(forward_kernel, layer),
            [full, narrow, half, half],
            scratch,
            (x, *terms, *loaded),
        )
        saved.append((x, inner))
    terms, loaded, _, _ = sum_mp(ta, tb, weights(3))
    x, inner, inner_grad, ta, tb = call(
        functools.partial(turn_kernel, 3),
        [full, narrow, hid, half, half],
        scratch,
        (x, *terms, g, *loaded),
    )
    grad_b = g
    for layer in (3, 2, 1):
        keep, send = weight_terms(layer, tables[layer], inner_grad, inner, x, grad_b)
        first, second = [keep], [swap(send, "seq", 1)]
        if layer == 1:
            three_kept, three_sent = halved(three_kept, three_got)
            second += [swap(three_sent, "seq", 24), swap(two_sent, "seq", 8)]
        if layer == 2:
            second += [swap(three_sent, "seq", 8)]
        terms, loaded, (keep,), (other, *rest) = sum_mp(ta, tb, weights(layer - 1), first, second)
        kept, sent = merge(keep, other, 2)
        if layer == 3:
            three_kept, three_sent = kept, sent
        if layer == 2:
            (three_got,) = rest
            two_kept, two_sent = kept, sent
        if layer == 1:
            three_got, two_got = rest
        above, (x, inner) = x, saved[layer - 1]
        if layer > 1:
            g, grad_b, inner_grad, ta, tb = call(
                functools.partial(backward_kernel, layer - 1),
                [struct((ROWS, C), F32), full, hid, half, half],
                [],
                (g, *terms, above, inner, *loaded),
            )
    two_kept, two_sent = halved(two_kept, two_got)
    a, kept, sent, two_kept, two_sent = together(terms[0], kept, sent, two_kept, two_sent)
    terms = (a, *terms[1:])
    grad_b, inner_grad, sent_blocks = call(
        final_kernel,
        [full, hid, struct((512, H), BF16)],
        [],
        (me, g, *terms, above, inner, block_go, loaded[1]),
        {0: pltpu.SMEM},
    )
    got = lax.all_to_all(sent_blocks.reshape(PEERS, 16, H), "seq", 0, 0)
    keep, send = weight_terms(0, tables[0], inner_grad, inner, x, grad_b)
    (first,) = merge(keep, swap(send, "seq", 1), 1)
    got, first, come, two_got = together(
        got, first, swap(sent, "seq", X), swap(two_sent, "seq", 3 * Z)
    )
    first = over_chips(first)
    kept, sent = halved(kept, come)
    come = swap(sent, "seq", 3 * X)
    late = [halved(two_kept, two_got), halved(three_kept, three_got)]
    late_kept, late_sent = (jnp.concatenate(parts, axis=0) for parts in zip(*late))
    got, late_come = together(got, swap(late_sent, "seq", X))
    late_kept, late_sent = (
        jnp.concatenate(
            [add(late_kept[n : n + 24], late_come[n : n + 24]) for n in (at, at + 48)], axis=0
        )
        for at in (0, 24)
    )
    late_come = swap(late_sent, "seq", 3 * X)
    piece = struct((ROWS, SHARD), BF16)
    total, one, three, two, gradient = call(
        last_kernel,
        [struct((ROWS, SHARD), F32), piece, piece, piece, struct((ROWS, SHARD), F32)],
        [pltpu.VMEM((ROWS, C), F32)],
        (me, got.reshape(512, H), block_come, loaded[0]),
        {0: pltpu.SMEM},
    )
    got = [swap(s, "mp", mask) for s, mask in ((one, 1), (three, 3), (two, 2))]
    for s in got:
        total = total + s.astype(F32)
    gradient = gradient + slope(inputs.astype(F32)) * total
    kept, sent = halved(kept, come)
    come = swap(sent, "seq", Z)
    kept, sent = halved(kept, come)
    come = swap(sent, "seq", 3 * Z)
    kernel_grad, point_grad = call(
        sums_kernel,
        [struct((3, 6, LAYERS, C), F32), struct((6, LAYERS, C), F32)],
        [],
        (first, kept, come, late_kept, late_come),
        flops=1e7,
    )
    return gradient, kernel_grad.transpose(2, 0, 1, 3), point_grad.transpose(1, 0, 2)


def solution(mesh):
    return jax.shard_map(
        shards,
        mesh=mesh,
        in_specs=(P("seq", "mp"), P("seq", "mp"), P(None, None, "mp", None), P(None, "mp", None)),
        out_specs=(
            P("seq", "mp"),
            P(None, None, ("mp", "seq"), None),
            P(None, ("mp", "seq"), None),
        ),
        check_vma=False,
    )
```

```python
import functools

import jax
import jax.numpy as jnp
import numpy as np
from jax import lax
from jax.experimental import pallas as pl
from jax.experimental.pallas import tpu as pltpu
from jax.sharding import PartitionSpec as P

LAYERS = 4
ROWS = 128
C = 1536
H = 192
HALF = C // 2
SHARD = C // 4
PEERS = 32
BF16 = jnp.bfloat16
F32 = jnp.float32
ORDER = (0, 3, 1, 2)
X, Z = 2, 8
ROOT = float(np.sqrt(2.0 / np.pi))
CUBE = 0.044715


def together(*values):
    return lax.optimization_barrier(values)


def dot(a, b, ca=1, cb=0):
    return lax.dot_general(a, b, (((ca,), (cb,)), ((), ())), preferred_element_type=F32)


def swap(values, axis, mask):
    peers = lax.axis_size(axis)
    return lax.ppermute(values, axis, [(i, i ^ mask) for i in range(peers)])


def add(a, b):
    return (a.astype(F32) + b.astype(F32)).astype(BF16)


def slope(x):
    square = x * x
    t = jnp.tanh(ROOT * x * (1.0 + CUBE * square))
    return 0.5 * (1.0 + t) + 0.5 * x * (1.0 - t * t) * (ROOT * (1.0 + 3.0 * CUBE * square))


def shifted(values, by):
    if by == 0:
        return values
    length = values.shape[0]
    zeros = jnp.zeros((abs(by),) + values.shape[1:], values.dtype)
    if by > 0:
        return jnp.concatenate([values[by:], zeros], axis=0)
    return jnp.concatenate([zeros, values[: length + by]], axis=0)


def struct(shape, kind):
    return jax.ShapeDtypeStruct(shape, kind)


def call(body, outs, scratch, args, spaces=None, flops=4e8):
    spaces = spaces or {}
    return pl.pallas_call(
        body,
        out_shape=outs,
        in_specs=[
            pl.BlockSpec(memory_space=spaces.get(i, pltpu.VMEM)) for i in range(len(args))
        ],
        out_specs=[pl.BlockSpec(memory_space=pltpu.VMEM)] * len(outs),
        scratch_shapes=scratch,
        compiler_params=pltpu.CompilerParams(vmem_limit_bytes=16 * 2**20),
        cost_estimate=pl.CostEstimate(flops=1000, bytes_accessed=1000, transcendentals=0),
    )(*args)


def chunks():
    return [slice(i, i + 16) for i in range(0, ROWS, 16)]


def total_of(rows, half, first, second):
    a, b = (first, second)[half]
    return a[rows].astype(F32) + b[rows].astype(F32)


def conv(active, k_mem, distance):
    taps = [dot(active, k_mem[k], 1, 1) for k in range(3)]
    return taps[1] + shifted(taps[0], -distance) + shifted(taps[2], distance)


def conv_back(inner_grad, k_mem, distance):
    out = None
    for k in range(3):
        moved = shifted(inner_grad, (1 - k) * distance).astype(BF16)
        part = dot(moved, k_mem[k])
        out = part if out is None else out + part
    return out


def put_halves(term, ta, tb):
    term = term.astype(BF16)
    ta[...] = term[:, :HALF]
    tb[...] = term[:, HALF:]


def backward_of(inner, grad_b, p_mem):
    hidden_grad = dot(grad_b, p_mem[...], 1, 1)
    return (hidden_grad * slope(inner)).astype(BF16)


def start_kernel(me, own, one, three, two, k_mem, p_mem, *rest):
    x, g, inner, ta, tb, active = rest
    for mask, block in ((0, own), (1, one), (3, three), (2, two)):
        at = pl.ds(pl.multiple_of((me[0] ^ mask) * SHARD, 128), SHARD)
        x[:, at] = block[:ROWS]
        g[:, at] = block[ROWS:]
    for rows in chunks():
        active[rows] = jax.nn.gelu(x[rows].astype(F32)).astype(BF16)
    values = conv(active[...], k_mem, 1)
    inner[...] = values
    put_halves(dot(jax.nn.gelu(values).astype(BF16), p_mem[...]), ta, tb)


def forward_kernel(layer, x, a, b, a2, b2, k_mem, p_mem, *rest):
    x1, inner, ta, tb, active = rest
    advance(x, a, b, a2, b2, x1, active)
    values = conv(active[...], k_mem, 2**layer)
    inner[...] = values
    put_halves(dot(jax.nn.gelu(values).astype(BF16), p_mem[...]), ta, tb)


def advance(x, a, b, a2, b2, x1, active):
    for rows in chunks():
        for half in (0, 1):
            at = slice(half * HALF, half * HALF + HALF)
            total = total_of(rows, half, (a, a2), (b, b2))
            values = (x[rows, at].astype(F32) + total).astype(BF16)
            x1[rows, at] = values
            active[rows, at] = jax.nn.gelu(values.astype(F32)).astype(BF16)


def turn_kernel(layer, x, a, b, a2, b2, g, k_mem, p_mem, *rest):
    x1, inner, inner_grad, ta, tb, active = rest
    advance(x, a, b, a2, b2, x1, active)
    before = conv(active[...], k_mem, 2**layer)
    inner[...] = before
    values = backward_of(before, g[...], p_mem)
    inner_grad[...] = values
    put_halves(conv_back(values.astype(F32), k_mem, 2**layer), ta, tb)


def retreat(g, a, b, a2, b2, x, g1, grad_b):
    for rows in chunks():
        for half in (0, 1):
            at = slice(half * HALF, half * HALF + HALF)
            total = total_of(rows, half, (a, a2), (b, b2))
            values = g[rows, at].astype(F32) + slope(x[rows, at].astype(F32)) * total
            if g1 is not None:
                g1[rows, at] = values
            grad_b[rows, at] = values.astype(BF16)


def backward_kernel(layer, g, a, b, a2, b2, x, inner, k_mem, p_mem, *rest):
    g1, grad_b, inner_grad, ta, tb = rest
    retreat(g, a, b, a2, b2, x, g1, grad_b)
    values = backward_of(inner[...], grad_b[...], p_mem)
    inner_grad[...] = values
    put_halves(conv_back(values.astype(F32), k_mem, 2**layer), ta, tb)


def final_kernel(me, g, a, b, a2, b2, x, inner, order, p_mem, *rest):
    grad_b, inner_grad, sent = rest
    retreat(g, a, b, a2, b2, x, None, grad_b)
    values = backward_of(inner[...], grad_b[...], p_mem)
    inner_grad[...] = values
    own = grad_b[:, pl.ds(pl.multiple_of(me[0] * SHARD, 128), SHARD)]
    parts = jnp.concatenate([values, own[:, :H], own[:, H:]], axis=0)
    sent[...] = dot(order[...], parts).astype(BF16)


def last_kernel(me, got, order, k_mem, *rest):
    own, one, three, two, g, term = rest
    values = dot(order[...], got[...])
    moved = values.astype(BF16)
    g[:, :H] = values[192:320]
    g[:, H:] = values[320:448]
    out = dot(moved[64:192], k_mem[0])
    out = out + dot(moved[32:160], k_mem[1])
    term[...] = out + dot(moved[:128], k_mem[2])
    for mask, ref in ((0, own), (1, one), (3, three), (2, two)):
        at = pl.ds(pl.multiple_of((me[0] ^ mask) * SHARD, 128), SHARD)
        ref[...] = term[:, at].astype(ref.dtype)


def weight_kernel(distance, inner_grad, inner, x, grad_b, table, keep, send):
    grad = inner_grad[...].astype(F32)
    top = None
    for k in range(3):
        moved = shifted(grad, (1 - k) * distance).astype(BF16)
        part = dot(moved, table[k * H : (k + 1) * H])
        top = part if top is None else top + part
    bottom = dot(jax.nn.gelu(inner[...]).astype(BF16), table[3 * H :])
    left = jnp.concatenate([top, bottom], axis=0).T.astype(BF16)
    for column in range(0, C, 384):
        at = slice(column, column + 384)
        active = jax.nn.gelu(x[:, at].astype(F32)).astype(BF16)
        right = jnp.concatenate([active, grad_b[:, at]], axis=0)
        for ref, row in ((keep, 0), (send, 384)):
            ref[:, at] = dot(left[row : row + 384], right).astype(BF16)


def weight_terms(layer, table, inner_grad, inner, x, grad_b):
    body = functools.partial(weight_kernel, 2**layer)
    outs = [struct((384, C), BF16)] * 2
    return call(body, outs, [], (inner_grad, inner, x, grad_b, table), flops=8e8)


def merge_kernel(kept, other, *outs):
    size = outs[0].shape[0]
    for number, out in enumerate(outs):
        rows = slice(size * number, size * number + size)
        out[...] = add(kept[rows], other[rows])


def merge(kept, other, count):
    return call(
        merge_kernel, [struct((384 // count, C), BF16)] * count, [], (kept, other), flops=1e7
    )


def sums_kernel(first, kept, come, late_kept, late_come, kernel_out, point_out):
    total = first[0].astype(F32)
    for i in range(1, 16):
        total = total + first[i].astype(F32)
    second = kept[...].astype(F32) + come[...].astype(F32)
    late = late_kept[...].astype(F32) + late_come[...].astype(F32)
    layers = (total, second, late[:24], late[24:])
    for row in range(24):
        values = jnp.concatenate([v[row : row + 1] for v in layers], axis=0)
        if row < 18:
            kernel_out[row // 6, row % 6] = values
        else:
            point_out[row - 18] = values


def table_of(source, columns):
    (source,) = together(jnp.asarray(source, jnp.int32))
    return (lax.broadcasted_iota(jnp.int32, (len(source), columns), 1) == source[:, None]).astype(
        BF16
    )


def by_source(blocks):
    column = np.arange(768)
    row = column % 24
    (source,) = together(jnp.asarray(row // 6 * H + row % 6, jnp.int32) + 6 * blocks)
    return (lax.broadcasted_iota(jnp.int32, (768, 768), 0) == source[None]).astype(BF16)


def absolute_order():
    core = lax.axis_index("seq") % 2
    block = np.arange(768) // 24
    return by_source(
        jnp.asarray(2 * (block % 16), jnp.int32) + (core ^ jnp.asarray(block // 16, jnp.int32))
    )


def relative_order(outer, inner):
    me = lax.axis_index("seq")
    masks = [c + outer * i + inner * j for c in (0, 1) for i in ORDER for j in ORDER]
    return by_source(me ^ jnp.asarray(np.repeat(masks, 24), jnp.int32))


def block_to_residue():
    n = np.arange(256)
    r, t = n // 8, n % 8
    go = t // 4 * 128 + t % 4 * 32 + r
    come = n % 128 // 4 * 8 + n // 128 * 4 + n % 4
    return table_of(go, 256), table_of(come, 256)


def residue_to_block():
    n = np.arange(512)
    s, t = n // 16, n % 16
    a = 4 * s + t - 1
    grad = np.where((t < 6) & (a >= 0) & (a < 128), a, -1)
    half = 128 + (t - 6) // 4 * 128 + 4 * s + (t - 6) % 4
    go = np.where(t < 6, grad, np.where(t < 14, half, -1))
    n = np.arange(448)
    m = n - 192
    come = np.where(
        n < 192, n % 32 * 16 + n // 32, m % 32 * 16 + 6 + m // 128 * 4 + m % 128 // 32
    )
    return table_of(go, 384), table_of(come, 512)


def halved(kept, come):
    rows = kept.shape[0] // 2
    return add(kept[:rows], come[:rows]), add(kept[rows:], come[rows:])


def over_chips(values):
    groups = [[2 * i + core for i in range(PEERS // 2)] for core in (0, 1)]
    return lax.all_to_all(
        values.reshape(16, 24, values.shape[1]), "seq", 0, 0, axis_index_groups=groups
    )


def sum_mp(a, b, load, first=(), second=()):
    a1, b1, *first = together(swap(a, "mp", 1), swap(b, "mp", 3), *first)
    a, b = add(a, a1), add(b, b1)
    loaded = load(a)
    a2, b2, *rest = together(swap(a, "mp", 3), swap(b, "mp", 1), *second, *loaded)
    return (a, b, a2, b2), rest[len(second) :], first, rest[: len(second)]


def shards(inputs, cotangent, conv_kernels, point_weights):
    me = lax.axis_index("mp").astype(jnp.int32)[None]

    def weights(layer):
        def load(after):
            _, kernels, points = together(after, conv_kernels, point_weights)
            return kernels[layer], points[layer]

        return load

    go, come = block_to_residue()
    sent = dot(go, jnp.concatenate([inputs, cotangent], axis=0)).astype(BF16)
    got = lax.all_to_all(sent.reshape(PEERS, 8, SHARD), "seq", 0, 0)
    own = dot(come, got.reshape(256, SHARD)).astype(BF16)
    loaded = weights(0)(own)
    one, three, two, *loaded = together(*[swap(own, "mp", mask) for mask in (1, 3, 2)], *loaded)
    full, narrow, hid = struct((ROWS, C), BF16), struct((ROWS, H), F32), struct((ROWS, H), BF16)
    half = struct((ROWS, HALF), BF16)
    scratch = [pltpu.VMEM((ROWS, C), BF16)]
    x, g, inner, ta, tb = call(
        start_kernel,
        [full, full, narrow, half, half],
        scratch,
        (me, own, one, three, two, *loaded),
        {0: pltpu.SMEM},
    )
    saved = [(x, inner)]
    tables = {2: relative_order(Z, X), 1: relative_order(X, Z), 0: absolute_order()}
    tables[3] = tables[2]
    block_go, block_come = residue_to_block()
    for layer in (1, 2):
        terms, loaded, _, _ = sum_mp(ta, tb, weights(layer))
        x, inner, ta, tb = call(
            functools.partial(forward_kernel, layer),
            [full, narrow, half, half],
            scratch,
            (x, *terms, *loaded),
        )
        saved.append((x, inner))
    terms, loaded, _, _ = sum_mp(ta, tb, weights(3))
    x, inner, inner_grad, ta, tb = call(
        functools.partial(turn_kernel, 3),
        [full, narrow, hid, half, half],
        scratch,
        (x, *terms, g, *loaded),
    )
    grad_b = g
    for layer in (3, 2, 1):
        keep, send = weight_terms(layer, tables[layer], inner_grad, inner, x, grad_b)
        first, second = [keep], [swap(send, "seq", 1)]
        if layer == 1:
            second = [*merge(keep, second[0], 2)]
        if layer == 1:
            three_kept, three_sent = halved(three_kept, three_got)
            second += [swap(three_sent, "seq", 24), swap(two_sent, "seq", 8)]
        if layer == 2:
            second += [swap(three_sent, "seq", 8)]
        terms, loaded, (keep,), (other, *rest) = sum_mp(ta, tb, weights(layer - 1), first, second)
        if layer > 1:
            kept, sent = merge(keep, other, 2)
        if layer == 3:
            three_kept, three_sent = kept, sent
        if layer == 2:
            (three_got,) = rest
            two_kept, two_sent = kept, sent
        if layer == 1:
            kept = other
            sent, three_got, two_got = rest
        above, (x, inner) = x, saved[layer - 1]
        if layer > 1:
            g, grad_b, inner_grad, ta, tb = call(
                functools.partial(backward_kernel, layer - 1),
                [struct((ROWS, C), F32), full, hid, half, half],
                [],
                (g, *terms, above, inner, *loaded),
            )
    two_kept, two_sent = halved(two_kept, two_got)
    grad_b, inner_grad, sent_blocks = call(
        final_kernel,
        [full, hid, struct((512, H), BF16)],
        [],
        (me, g, *terms, above, inner, block_go, loaded[1]),
        {0: pltpu.SMEM},
    )
    got = lax.all_to_all(sent_blocks.reshape(PEERS, 16, H), "seq", 0, 0)
    come = swap(sent, "seq", X)
    inner_grad, two_got = together(inner_grad, swap(two_sent, "seq", 3 * Z))
    keep, send = weight_terms(0, tables[0], inner_grad, inner, x, grad_b)
    (first,) = merge(keep, swap(send, "seq", 1), 1)
    late = [halved(two_kept, two_got), halved(three_kept, three_got)]
    late = [jnp.concatenate(parts, axis=0) for parts in zip(*late)]
    got, first, kept, sent, late_kept, late_sent = together(got, first, *halved(kept, come), *late)
    first = over_chips(first)
    come = swap(sent, "seq", 3 * X)
    got, late_come = together(got, swap(late_sent, "seq", X))
    late_kept, late_sent = (
        jnp.concatenate(
            [add(late_kept[n : n + 24], late_come[n : n + 24]) for n in (at, at + 48)], axis=0
        )
        for at in (0, 24)
    )
    late_come = swap(late_sent, "seq", 3 * X)
    piece = struct((ROWS, SHARD), BF16)
    total, one, three, two, gradient = call(
        last_kernel,
        [struct((ROWS, SHARD), F32), piece, piece, piece, struct((ROWS, SHARD), F32)],
        [pltpu.VMEM((ROWS, C), F32)],
        (me, got.reshape(512, H), block_come, loaded[0]),
        {0: pltpu.SMEM},
    )
    got = [swap(s, "mp", mask) for s, mask in ((one, 1), (three, 3), (two, 2))]
    for s in got:
        total = total + s.astype(F32)
    gradient = gradient + slope(inputs.astype(F32)) * total
    kept, sent = halved(kept, come)
    come = swap(sent, "seq", Z)
    kept, sent = halved(kept, come)
    come = swap(sent, "seq", 3 * Z)
    kernel_grad, point_grad = call(
        sums_kernel,
        [struct((3, 6, LAYERS, C), F32), struct((6, LAYERS, C), F32)],
        [],
        (first, kept, come, late_kept, late_come),
        flops=1e7,
    )
    return gradient, kernel_grad.transpose(2, 0, 1, 3), point_grad.transpose(1, 0, 2)


def solution(mesh):
    return jax.shard_map(
        shards,
        mesh=mesh,
        in_specs=(P("seq", "mp"), P("seq", "mp"), P(None, None, "mp", None), P(None, "mp", None)),
        out_specs=(
            P("seq", "mp"),
            P(None, None, ("mp", "seq"), None),
            P(None, ("mp", "seq"), None),
        ),
        check_vma=False,
    )
```

```python
import functools

import jax
import jax.numpy as jnp
import numpy as np
from jax import lax
from jax.experimental import pallas as pl
from jax.experimental.pallas import tpu as pltpu
from jax.sharding import PartitionSpec as P

LAYERS = 4
ROWS = 128
C = 1536
H = 192
HALF = C // 2
SHARD = C // 4
PEERS = 32
BF16 = jnp.bfloat16
F32 = jnp.float32
ORDER = (0, 3, 1, 2)
X, Z = 2, 8
ROOT = float(np.sqrt(2.0 / np.pi))
CUBE = 0.044715


def together(*values):
    return lax.optimization_barrier(values)


def dot(a, b, ca=1, cb=0):
    return lax.dot_general(a, b, (((ca,), (cb,)), ((), ())), preferred_element_type=F32)


def swap(values, axis, mask):
    peers = lax.axis_size(axis)
    return lax.ppermute(values, axis, [(i, i ^ mask) for i in range(peers)])


def add(a, b):
    return (a.astype(F32) + b.astype(F32)).astype(BF16)


def slope(x):
    square = x * x
    t = jnp.tanh(ROOT * x * (1.0 + CUBE * square))
    return 0.5 * (1.0 + t) + 0.5 * x * (1.0 - t * t) * (ROOT * (1.0 + 3.0 * CUBE * square))


def shifted(values, by):
    if by == 0:
        return values
    length = values.shape[0]
    zeros = jnp.zeros((abs(by),) + values.shape[1:], values.dtype)
    if by > 0:
        return jnp.concatenate([values[by:], zeros], axis=0)
    return jnp.concatenate([zeros, values[: length + by]], axis=0)


def struct(shape, kind):
    return jax.ShapeDtypeStruct(shape, kind)


def call(body, outs, scratch, args, spaces=None, flops=4e8):
    spaces = spaces or {}
    return pl.pallas_call(
        body,
        out_shape=outs,
        in_specs=[
            pl.BlockSpec(memory_space=spaces.get(i, pltpu.VMEM)) for i in range(len(args))
        ],
        out_specs=[pl.BlockSpec(memory_space=pltpu.VMEM)] * len(outs),
        scratch_shapes=scratch,
        compiler_params=pltpu.CompilerParams(vmem_limit_bytes=16 * 2**20),
        cost_estimate=pl.CostEstimate(flops=1000, bytes_accessed=1000, transcendentals=0),
    )(*args)


def chunks():
    return [slice(i, i + 16) for i in range(0, ROWS, 16)]


def total_of(rows, half, first, second):
    a, b = (first, second)[half]
    return a[rows].astype(F32) + b[rows].astype(F32)


def conv(active, k_mem, distance):
    taps = [dot(active, k_mem[k], 1, 1) for k in range(3)]
    return taps[1] + shifted(taps[0], -distance) + shifted(taps[2], distance)


def conv_back(inner_grad, k_mem, distance):
    out = None
    for k in range(3):
        moved = shifted(inner_grad, (1 - k) * distance).astype(BF16)
        part = dot(moved, k_mem[k])
        out = part if out is None else out + part
    return out


def put_halves(term, ta, tb):
    term = term.astype(BF16)
    ta[...] = term[:, :HALF]
    tb[...] = term[:, HALF:]


def backward_of(inner, grad_b, p_mem):
    hidden_grad = dot(grad_b, p_mem[...], 1, 1)
    return (hidden_grad * slope(inner)).astype(BF16)


def start_kernel(me, own, one, three, two, k_mem, p_mem, *rest):
    x, g, inner, ta, tb, active = rest
    for mask, block in ((0, own), (1, one), (3, three), (2, two)):
        at = pl.ds(pl.multiple_of((me[0] ^ mask) * SHARD, 128), SHARD)
        x[:, at] = block[:ROWS]
        g[:, at] = block[ROWS:]
    for rows in chunks():
        active[rows] = jax.nn.gelu(x[rows].astype(F32)).astype(BF16)
    values = conv(active[...], k_mem, 1)
    inner[...] = values
    put_halves(dot(jax.nn.gelu(values).astype(BF16), p_mem[...]), ta, tb)


def forward_kernel(layer, x, a, b, a2, b2, k_mem, p_mem, *rest):
    x1, inner, ta, tb, active = rest
    advance(x, a, b, a2, b2, x1, active)
    values = conv(active[...], k_mem, 2**layer)
    inner[...] = values
    put_halves(dot(jax.nn.gelu(values).astype(BF16), p_mem[...]), ta, tb)


def advance(x, a, b, a2, b2, x1, active):
    for rows in chunks():
        for half in (0, 1):
            at = slice(half * HALF, half * HALF + HALF)
            total = total_of(rows, half, (a, a2), (b, b2))
            values = (x[rows, at].astype(F32) + total).astype(BF16)
            x1[rows, at] = values
            active[rows, at] = jax.nn.gelu(values.astype(F32)).astype(BF16)


def turn_kernel(layer, x, a, b, a2, b2, g, k_mem, p_mem, *rest):
    x1, inner, inner_grad, ta, tb, active = rest
    advance(x, a, b, a2, b2, x1, active)
    before = conv(active[...], k_mem, 2**layer)
    inner[...] = before
    values = backward_of(before, g[...], p_mem)
    inner_grad[...] = values
    put_halves(conv_back(values.astype(F32), k_mem, 2**layer), ta, tb)


def retreat(g, a, b, a2, b2, x, g1, grad_b):
    for rows in chunks():
        for half in (0, 1):
            at = slice(half * HALF, half * HALF + HALF)
            total = total_of(rows, half, (a, a2), (b, b2))
            values = g[rows, at].astype(F32) + slope(x[rows, at].astype(F32)) * total
            g1[rows, at] = values
            grad_b[rows, at] = values.astype(BF16)


def backward_kernel(layer, g, a, b, a2, b2, x, inner, k_mem, p_mem, *rest):
    g1, grad_b, inner_grad, ta, tb = rest
    retreat(g, a, b, a2, b2, x, g1, grad_b)
    values = backward_of(inner[...], grad_b[...], p_mem)
    inner_grad[...] = values
    put_halves(conv_back(values.astype(F32), k_mem, 2**layer), ta, tb)


def final_kernel(me, g, a, b, a2, b2, x, first, inner, k_mem, p_mem, *rest):
    grad_b, inner_grad, own, one, three, two, base, rate, term, g1 = rest
    retreat(g, a, b, a2, b2, x, g1, grad_b)
    at = pl.ds(pl.multiple_of(me[0] * SHARD, 128), SHARD)
    rate[...] = slope(first[:, at].astype(F32))
    values = backward_of(inner[...], grad_b[...], p_mem)
    inner_grad[...] = values
    term[...] = conv_back(values.astype(F32), k_mem, 1)
    for mask, ref in ((0, own), (1, one), (3, three), (2, two)):
        at = pl.ds(pl.multiple_of((me[0] ^ mask) * SHARD, 128), SHARD)
        ref[...] = term[:, at].astype(ref.dtype)
    base[...] = g1[:, pl.ds(pl.multiple_of(me[0] * SHARD, 128), SHARD)]


def pack_kernel(own, one, three, two, base, rate, order, keep, send):
    total = own[...]
    for ref in (one, three, two):
        total = total + ref[...].astype(F32)
    values = (base[...] + rate[...] * total).astype(BF16)
    values = dot(order[...], values).astype(BF16)
    for part, ref in enumerate((keep, send)):
        for t in range(4):
            rows = slice(32 * t + 16 * part, 32 * t + 16 * part + 16)
            ref[:, t * SHARD : (t + 1) * SHARD] = values[rows]


def weight_kernel(distance, inner_grad, inner, x, grad_b, table, keep, send):
    grad = inner_grad[...].astype(F32)
    top = None
    for k in range(3):
        moved = shifted(grad, (1 - k) * distance).astype(BF16)
        part = dot(moved, table[k * H : (k + 1) * H])
        top = part if top is None else top + part
    bottom = dot(jax.nn.gelu(inner[...]).astype(BF16), table[3 * H :])
    left = jnp.concatenate([top, bottom], axis=0).T.astype(BF16)
    for column in range(0, C, 384):
        at = slice(column, column + 384)
        active = jax.nn.gelu(x[:, at].astype(F32)).astype(BF16)
        right = jnp.concatenate([active, grad_b[:, at]], axis=0)
        for ref, row in ((keep, 0), (send, 384)):
            ref[:, at] = dot(left[row : row + 384], right).astype(BF16)


def weight_terms(layer, table, inner_grad, inner, x, grad_b):
    body = functools.partial(weight_kernel, 2**layer)
    outs = [struct((384, C), BF16)] * 2
    return call(body, outs, [], (inner_grad, inner, x, grad_b, table), flops=8e8)


def merge_kernel(kept, other, *outs):
    size = outs[0].shape[0]
    for number, out in enumerate(outs):
        rows = slice(size * number, size * number + size)
        out[...] = add(kept[rows], other[rows])


def merge(kept, other, count):
    return call(
        merge_kernel, [struct((384 // count, C), BF16)] * count, [], (kept, other), flops=1e7
    )


def exchange_kernel(kept, other, mine, sibling, out):
    total = kept[...].astype(F32) + other[...].astype(F32)
    mine, sibling = mine[...].astype(F32), sibling[...].astype(F32)
    for chip in range(16):
        parts = [total[24 * chip : 24 * chip + 24], mine[chip : chip + 1], sibling[chip : chip + 1]]
        out[chip] = jnp.concatenate([*parts, jnp.zeros((6, C), F32)], axis=0).astype(BF16)


def sums_kernel(first, kept, come, late_kept, late_come, order, gradient, kernel_out, point_out):
    total = first[0].astype(F32)
    ends = [total[24:]]
    for i in range(1, 16):
        part = first[i].astype(F32)
        ends.append(part[24:])
        total = total + part
    ends = [jnp.concatenate([e[n : n + 1] for e in ends], axis=0) for n in (0, 1)]
    ends = jnp.concatenate(ends, axis=0).astype(BF16)
    for t in range(4):
        rows = slice(32 * t, 32 * t + 32)
        gradient[rows] = dot(order[...], ends[:, t * SHARD : (t + 1) * SHARD])
    second = kept[...].astype(F32) + come[...].astype(F32)
    late = late_kept[...].astype(F32) + late_come[...].astype(F32)
    layers = (total[:24], second, late[:24], late[24:])
    for row in range(24):
        values = jnp.concatenate([v[row : row + 1] for v in layers], axis=0)
        if row < 18:
            kernel_out[row // 6, row % 6] = values
        else:
            point_out[row - 18] = values


def table_of(source, columns):
    (source,) = together(jnp.asarray(source, jnp.int32))
    return (lax.broadcasted_iota(jnp.int32, (len(source), columns), 1) == source[:, None]).astype(
        BF16
    )


def by_source(blocks):
    column = np.arange(768)
    row = column % 24
    (source,) = together(jnp.asarray(row // 6 * H + row % 6, jnp.int32) + 6 * blocks)
    return (lax.broadcasted_iota(jnp.int32, (768, 768), 0) == source[None]).astype(BF16)


def absolute_order():
    core = lax.axis_index("seq") % 2
    block = np.arange(768) // 24
    return by_source(
        jnp.asarray(2 * (block % 16), jnp.int32) + (core ^ jnp.asarray(block // 16, jnp.int32))
    )


def relative_order(outer, inner):
    me = lax.axis_index("seq")
    masks = [c + outer * i + inner * j for c in (0, 1) for i in ORDER for j in ORDER]
    return by_source(me ^ jnp.asarray(np.repeat(masks, 24), jnp.int32))


def block_to_residue():
    n = np.arange(256)
    r, t = n // 8, n % 8
    go = t // 4 * 128 + t % 4 * 32 + r
    come = n % 128 // 4 * 8 + n // 128 * 4 + n % 4
    return table_of(go, 256), table_of(come, 256)


def residue_to_block():
    core = lax.axis_index("seq") % 2
    n = np.arange(32)
    device = jnp.asarray(2 * (n % 16), jnp.int32) + (core ^ jnp.asarray(n // 16, jnp.int32))
    go = (4 * device[None] + jnp.arange(4, dtype=jnp.int32)[:, None]).reshape(128)
    (go, device) = together(go, device)
    go = lax.broadcasted_iota(jnp.int32, (128, 128), 1) == go[:, None]
    come = lax.broadcasted_iota(jnp.int32, (32, 32), 0) == device[None]
    return go.astype(BF16), come.astype(BF16)


def halved(kept, come):
    rows = kept.shape[0] // 2
    return add(kept[:rows], come[:rows]), add(kept[rows:], come[rows:])


def over_chips(values):
    groups = [[2 * i + core for i in range(PEERS // 2)] for core in (0, 1)]
    return lax.all_to_all(values, "seq", 0, 0, axis_index_groups=groups)


def sum_mp(a, b, load, first=(), second=()):
    a1, b1 = swap(a, "mp", 1), swap(b, "mp", 3)
    if first:
        a1, b1, *first = together(a1, b1, *first)
    else:
        _, b1 = together(a1, b1)
    a, b = add(a, a1), add(b, b1)
    loaded = load(a) if first else load(a, b)
    a2, b2, *rest = together(swap(a, "mp", 3), swap(b, "mp", 1), *second, *loaded)
    return (a, b, a2, b2), rest[len(second) :], first, rest[: len(second)]


def shards(inputs, cotangent, conv_kernels, point_weights):
    me = lax.axis_index("mp").astype(jnp.int32)[None]

    def weights(layer):
        def load(*after):
            *_, kernels, points = together(*after, conv_kernels, point_weights)
            return kernels[layer], points[layer]

        return load

    go, come = block_to_residue()
    sent = dot(go, jnp.concatenate([inputs, cotangent], axis=0)).astype(BF16)
    got = lax.all_to_all(sent.reshape(PEERS, 8, SHARD), "seq", 0, 0)
    own = dot(come, got.reshape(256, SHARD)).astype(BF16)
    loaded = weights(0)(own)
    one, three, two, *loaded = together(*[swap(own, "mp", mask) for mask in (1, 3, 2)], *loaded)
    full, narrow, hid = struct((ROWS, C), BF16), struct((ROWS, H), F32), struct((ROWS, H), BF16)
    half = struct((ROWS, HALF), BF16)
    scratch = [pltpu.VMEM((ROWS, C), BF16)]
    x, g, inner, ta, tb = call(
        start_kernel,
        [full, full, narrow, half, half],
        scratch,
        (me, own, one, three, two, *loaded),
        {0: pltpu.SMEM},
    )
    saved = [(x, inner)]
    tables = {2: relative_order(Z, X), 1: relative_order(X, Z), 0: absolute_order()}
    tables[3] = tables[2]
    block_go, block_come = residue_to_block()
    for layer in (1, 2):
        terms, loaded, _, _ = sum_mp(ta, tb, weights(layer))
        x, inner, ta, tb = call(
            functools.partial(forward_kernel, layer),
            [full, narrow, half, half],
            scratch,
            (x, *terms, *loaded),
        )
        saved.append((x, inner))
    terms, loaded, _, _ = sum_mp(ta, tb, weights(3))
    x, inner, inner_grad, ta, tb = call(
        functools.partial(turn_kernel, 3),
        [full, narrow, hid, half, half],
        scratch,
        (x, *terms, g, *loaded),
    )
    grad_b = g
    for layer in (3, 2, 1):
        keep, send = weight_terms(layer, tables[layer], inner_grad, inner, x, grad_b)
        first, second = [keep], [swap(send, "seq", 1)]
        if layer == 1:
            second = [*merge(keep, second[0], 2)]
        if layer == 1:
            three_kept, three_sent = halved(three_kept, three_got)
            second += [swap(three_sent, "seq", 24), swap(two_sent, "seq", 8)]
        if layer == 2:
            second += [swap(three_sent, "seq", 8)]
        terms, loaded, (keep,), (other, *rest) = sum_mp(ta, tb, weights(layer - 1), first, second)
        if layer > 1:
            kept, sent = merge(keep, other, 2)
        if layer == 3:
            three_kept, three_sent = kept, sent
        if layer == 2:
            (three_got,) = rest
            two_kept, two_sent = kept, sent
        if layer == 1:
            kept = other
            sent, three_got, two_got = rest
        above, (x, inner) = x, saved[layer - 1]
        if layer > 1:
            g, grad_b, inner_grad, ta, tb = call(
                functools.partial(backward_kernel, layer - 1),
                [struct((ROWS, C), F32), full, hid, half, half],
                [],
                (g, *terms, above, inner, *loaded),
            )
    two_kept, two_sent = halved(two_kept, two_got)
    piece, wide = struct((ROWS, SHARD), BF16), struct((ROWS, SHARD), F32)
    grad_b, inner_grad, own, *pieces, base, rate = call(
        final_kernel,
        [full, hid, wide, piece, piece, piece, wide, wide],
        [pltpu.VMEM((ROWS, C), F32), pltpu.VMEM((ROWS, C), F32)],
        (me, g, *terms, above, x, inner, *loaded),
        {0: pltpu.SMEM},
    )
    come = swap(sent, "seq", X)
    pieces = [swap(s, "mp", mask) for s, mask in zip(pieces, (1, 3, 2))]
    two_got = swap(two_sent, "seq", 3 * Z)
    keep, send = weight_terms(0, tables[0], inner_grad, inner, x, grad_b)
    other = swap(send, "seq", 1)
    mine, send = call(
        pack_kernel,
        [struct((16, C), BF16)] * 2,
        [],
        (own, *pieces, base, rate, block_go),
        flops=1e7,
    )
    late = [halved(two_kept, two_got), halved(three_kept, three_got)]
    late = [jnp.concatenate(parts, axis=0) for parts in zip(*late)]
    sibling = swap(send, "seq", 1)
    kept, sent = halved(kept, come)
    late_kept, late_sent = late
    first = call(
        exchange_kernel, [struct((16, 32, C), BF16)], [], (keep, other, mine, sibling), flops=1e7
    )[0]
    first = over_chips(first)
    come = swap(sent, "seq", 3 * X)
    late_come = swap(late_sent, "seq", X)
    late_kept, late_sent = (
        jnp.concatenate(
            [add(late_kept[n : n + 24], late_come[n : n + 24]) for n in (at, at + 48)], axis=0
        )
        for at in (0, 24)
    )
    late_come = swap(late_sent, "seq", 3 * X)
    kept, sent = halved(kept, come)
    come = swap(sent, "seq", Z)
    kept, sent = halved(kept, come)
    come = swap(sent, "seq", 3 * Z)
    gradient, kernel_grad, point_grad = call(
        sums_kernel,
        [wide, struct((3, 6, LAYERS, C), F32), struct((6, LAYERS, C), F32)],
        [],
        (first, kept, come, late_kept, late_come, block_come),
        flops=1e7,
    )
    return gradient, kernel_grad.transpose(2, 0, 1, 3), point_grad.transpose(1, 0, 2)


def solution(mesh):
    return jax.shard_map(
        shards,
        mesh=mesh,
        in_specs=(P("seq", "mp"), P("seq", "mp"), P(None, None, "mp", None), P(None, "mp", None)),
        out_specs=(
            P("seq", "mp"),
            P(None, None, ("mp", "seq"), None),
            P(None, ("mp", "seq"), None),
        ),
        check_vma=False,
    )
```

```python
import functools

import jax
import jax.numpy as jnp
import numpy as np
from jax import lax
from jax.experimental import pallas as pl
from jax.experimental.pallas import tpu as pltpu
from jax.sharding import PartitionSpec as P

LAYERS = 4
ROWS = 128
C = 1536
H = 192
HALF = C // 2
SHARD = C // 4
PEERS = 32
BF16 = jnp.bfloat16
F32 = jnp.float32
ORDER = (0, 3, 1, 2)
X, Z = 2, 8
ROOT = float(np.sqrt(2.0 / np.pi))
CUBE = 0.044715


def together(*values):
    return lax.optimization_barrier(values)


def dot(a, b, ca=1, cb=0):
    return lax.dot_general(a, b, (((ca,), (cb,)), ((), ())), preferred_element_type=F32)


def swap(values, axis, mask):
    peers = lax.axis_size(axis)
    return lax.ppermute(values, axis, [(i, i ^ mask) for i in range(peers)])


def add(a, b):
    return (a.astype(F32) + b.astype(F32)).astype(BF16)


def slope(x):
    square = x * x
    t = jnp.tanh(ROOT * x * (1.0 + CUBE * square))
    return 0.5 * (1.0 + t) + 0.5 * x * (1.0 - t * t) * (ROOT * (1.0 + 3.0 * CUBE * square))


def shifted(values, by):
    if by == 0:
        return values
    length = values.shape[0]
    zeros = jnp.zeros((abs(by),) + values.shape[1:], values.dtype)
    if by > 0:
        return jnp.concatenate([values[by:], zeros], axis=0)
    return jnp.concatenate([zeros, values[: length + by]], axis=0)


def struct(shape, kind):
    return jax.ShapeDtypeStruct(shape, kind)


def call(body, outs, scratch, args, spaces=None, flops=4e8):
    spaces = spaces or {}
    return pl.pallas_call(
        body,
        out_shape=outs,
        in_specs=[
            pl.BlockSpec(memory_space=spaces.get(i, pltpu.VMEM)) for i in range(len(args))
        ],
        out_specs=[pl.BlockSpec(memory_space=pltpu.VMEM)] * len(outs),
        scratch_shapes=scratch,
        compiler_params=pltpu.CompilerParams(vmem_limit_bytes=16 * 2**20),
        cost_estimate=pl.CostEstimate(flops=1000, bytes_accessed=1000, transcendentals=0),
    )(*args)


def chunks():
    return [slice(i, i + 16) for i in range(0, ROWS, 16)]


def total_of(rows, half, first, second):
    a, b = (first, second)[half]
    return a[rows].astype(F32) + b[rows].astype(F32)


def conv(active, k_mem, distance):
    taps = [dot(active, k_mem[k], 1, 1) for k in range(3)]
    return taps[1] + shifted(taps[0], -distance) + shifted(taps[2], distance)


def conv_back(inner_grad, k_mem, distance):
    out = None
    for k in range(3):
        moved = shifted(inner_grad, (1 - k) * distance).astype(BF16)
        part = dot(moved, k_mem[k])
        out = part if out is None else out + part
    return out


def put_halves(term, ta, tb):
    term = term.astype(BF16)
    ta[...] = term[:, :HALF]
    tb[...] = term[:, HALF:]


def backward_of(inner, grad_b, p_mem):
    hidden_grad = dot(grad_b, p_mem[...], 1, 1)
    return (hidden_grad * slope(inner)).astype(BF16)


def start_kernel(me, own, one, three, two, k_mem, p_mem, *rest):
    x, inner, ta, tb, active = rest
    for mask, block in ((0, own), (1, one), (3, three), (2, two)):
        at = pl.ds(pl.multiple_of((me[0] ^ mask) * SHARD, 128), SHARD)
        x[:, at] = block[...]
    for rows in chunks():
        active[rows] = jax.nn.gelu(x[rows].astype(F32)).astype(BF16)
    values = conv(active[...], k_mem, 1)
    inner[...] = values
    put_halves(dot(jax.nn.gelu(values).astype(BF16), p_mem[...]), ta, tb)


def gather_kernel(me, own, one, three, two, out):
    for mask, block in ((0, own), (1, one), (3, three), (2, two)):
        at = pl.ds(pl.multiple_of((me[0] ^ mask) * SHARD, 128), SHARD)
        out[:, at] = block[...]


def forward_kernel(layer, x, a, b, a2, b2, k_mem, p_mem, *rest):
    x1, inner, ta, tb, active = rest
    advance(x, a, b, a2, b2, x1, active)
    values = conv(active[...], k_mem, 2**layer)
    inner[...] = values
    put_halves(dot(jax.nn.gelu(values).astype(BF16), p_mem[...]), ta, tb)


def advance(x, a, b, a2, b2, x1, active):
    for rows in chunks():
        for half in (0, 1):
            at = slice(half * HALF, half * HALF + HALF)
            total = total_of(rows, half, (a, a2), (b, b2))
            values = (x[rows, at].astype(F32) + total).astype(BF16)
            x1[rows, at] = values
            active[rows, at] = jax.nn.gelu(values.astype(F32)).astype(BF16)


def turn_kernel(layer, x, a, b, a2, b2, g, k_mem, p_mem, *rest):
    x1, inner, inner_grad, ta, tb, active = rest
    advance(x, a, b, a2, b2, x1, active)
    before = conv(active[...], k_mem, 2**layer)
    inner[...] = before
    values = backward_of(before, g[...], p_mem)
    inner_grad[...] = values
    put_halves(conv_back(values.astype(F32), k_mem, 2**layer), ta, tb)


def retreat(g, a, b, a2, b2, x, g1, grad_b):
    for rows in chunks():
        for half in (0, 1):
            at = slice(half * HALF, half * HALF + HALF)
            total = total_of(rows, half, (a, a2), (b, b2))
            values = g[rows, at].astype(F32) + slope(x[rows, at].astype(F32)) * total
            g1[rows, at] = values
            grad_b[rows, at] = values.astype(BF16)


def backward_kernel(layer, g, a, b, a2, b2, x, inner, k_mem, p_mem, *rest):
    g1, grad_b, inner_grad, ta, tb = rest
    retreat(g, a, b, a2, b2, x, g1, grad_b)
    values = backward_of(inner[...], grad_b[...], p_mem)
    inner_grad[...] = values
    put_halves(conv_back(values.astype(F32), k_mem, 2**layer), ta, tb)


def final_kernel(me, g, a, b, a2, b2, x, first, inner, k_mem, p_mem, *rest):
    grad_b, inner_grad, own, one, three, two, base, rate, term, g1 = rest
    retreat(g, a, b, a2, b2, x, g1, grad_b)
    at = pl.ds(pl.multiple_of(me[0] * SHARD, 128), SHARD)
    rate[...] = slope(first[:, at].astype(F32))
    values = backward_of(inner[...], grad_b[...], p_mem)
    inner_grad[...] = values
    term[...] = conv_back(values.astype(F32), k_mem, 1)
    for mask, ref in ((0, own), (1, one), (3, three), (2, two)):
        at = pl.ds(pl.multiple_of((me[0] ^ mask) * SHARD, 128), SHARD)
        ref[...] = term[:, at].astype(ref.dtype)
    base[...] = g1[:, pl.ds(pl.multiple_of(me[0] * SHARD, 128), SHARD)]


def pack_kernel(own, one, three, two, base, rate, order, keep, send):
    total = own[...]
    for ref in (one, three, two):
        total = total + ref[...].astype(F32)
    values = (base[...] + rate[...] * total).astype(BF16)
    values = dot(order[...], values).astype(BF16)
    for part, ref in enumerate((keep, send)):
        for t in range(4):
            rows = slice(32 * t + 16 * part, 32 * t + 16 * part + 16)
            ref[:, t * SHARD : (t + 1) * SHARD] = values[rows]


def weight_kernel(distance, inner_grad, inner, x, grad_b, table, keep, send):
    grad = inner_grad[...].astype(F32)
    top = None
    for k in range(3):
        moved = shifted(grad, (1 - k) * distance).astype(BF16)
        part = dot(moved, table[k * H : (k + 1) * H])
        top = part if top is None else top + part
    bottom = dot(jax.nn.gelu(inner[...]).astype(BF16), table[3 * H :])
    left = jnp.concatenate([top, bottom], axis=0).T.astype(BF16)
    for column in range(0, C, 384):
        at = slice(column, column + 384)
        active = jax.nn.gelu(x[:, at].astype(F32)).astype(BF16)
        right = jnp.concatenate([active, grad_b[:, at]], axis=0)
        for ref, row in ((keep, 0), (send, 384)):
            ref[:, at] = dot(left[row : row + 384], right).astype(BF16)


def weight_terms(layer, table, inner_grad, inner, x, grad_b):
    body = functools.partial(weight_kernel, 2**layer)
    outs = [struct((384, C), BF16)] * 2
    return call(body, outs, [], (inner_grad, inner, x, grad_b, table), flops=8e8)


def merge_kernel(kept, other, *outs):
    size = outs[0].shape[0]
    for number, out in enumerate(outs):
        rows = slice(size * number, size * number + size)
        out[...] = add(kept[rows], other[rows])


def merge(kept, other, count):
    return call(
        merge_kernel, [struct((384 // count, C), BF16)] * count, [], (kept, other), flops=1e7
    )


def exchange_kernel(kept, other, mine, sibling, out):
    total = kept[...].astype(F32) + other[...].astype(F32)
    mine, sibling = mine[...].astype(F32), sibling[...].astype(F32)
    for chip in range(16):
        parts = [total[24 * chip : 24 * chip + 24], mine[chip : chip + 1], sibling[chip : chip + 1]]
        out[chip] = jnp.concatenate([*parts, jnp.zeros((6, C), F32)], axis=0).astype(BF16)


def sums_kernel(first, kept, come, late_kept, late_come, order, gradient, kernel_out, point_out):
    total = first[0].astype(F32)
    ends = [total[24:]]
    for i in range(1, 16):
        part = first[i].astype(F32)
        ends.append(part[24:])
        total = total + part
    ends = [jnp.concatenate([e[n : n + 1] for e in ends], axis=0) for n in (0, 1)]
    ends = jnp.concatenate(ends, axis=0).astype(BF16)
    for t in range(4):
        rows = slice(32 * t, 32 * t + 32)
        gradient[rows] = dot(order[...], ends[:, t * SHARD : (t + 1) * SHARD])
    second = kept[...].astype(F32) + come[...].astype(F32)
    late = late_kept[...].astype(F32) + late_come[...].astype(F32)
    layers = (total[:24], second, late[:24], late[24:])
    for row in range(24):
        values = jnp.concatenate([v[row : row + 1] for v in layers], axis=0)
        if row < 18:
            kernel_out[row // 6, row % 6] = values
        else:
            point_out[row - 18] = values


def table_of(source, columns):
    (source,) = together(jnp.asarray(source, jnp.int32))
    return (lax.broadcasted_iota(jnp.int32, (len(source), columns), 1) == source[:, None]).astype(
        BF16
    )


def by_source(blocks):
    column = np.arange(768)
    row = column % 24
    (source,) = together(jnp.asarray(row // 6 * H + row % 6, jnp.int32) + 6 * blocks)
    return (lax.broadcasted_iota(jnp.int32, (768, 768), 0) == source[None]).astype(BF16)


def absolute_order():
    core = lax.axis_index("seq") % 2
    block = np.arange(768) // 24
    return by_source(
        jnp.asarray(2 * (block % 16), jnp.int32) + (core ^ jnp.asarray(block // 16, jnp.int32))
    )


def relative_order(outer, inner):
    me = lax.axis_index("seq")
    masks = [c + outer * i + inner * j for c in (0, 1) for i in ORDER for j in ORDER]
    return by_source(me ^ jnp.asarray(np.repeat(masks, 24), jnp.int32))


def block_to_residue():
    n = np.arange(256)
    r, t = n // 8, n % 8
    go = t // 4 * 128 + t % 4 * 32 + r
    come = n % 128 // 4 * 8 + n // 128 * 4 + n % 4
    return table_of(go, 256), table_of(come, 256)


def residue_to_block():
    core = lax.axis_index("seq") % 2
    n = np.arange(32)
    device = jnp.asarray(2 * (n % 16), jnp.int32) + (core ^ jnp.asarray(n // 16, jnp.int32))
    go = (4 * device[None] + jnp.arange(4, dtype=jnp.int32)[:, None]).reshape(128)
    (go, device) = together(go, device)
    go = lax.broadcasted_iota(jnp.int32, (128, 128), 1) == go[:, None]
    come = lax.broadcasted_iota(jnp.int32, (32, 32), 0) == device[None]
    return go.astype(BF16), come.astype(BF16)


def halved(kept, come):
    rows = kept.shape[0] // 2
    return add(kept[:rows], come[:rows]), add(kept[rows:], come[rows:])


def over_chips(values):
    groups = [[2 * i + core for i in range(PEERS // 2)] for core in (0, 1)]
    return lax.all_to_all(values, "seq", 0, 0, axis_index_groups=groups)


def sum_mp(a, b, load, first=(), second=()):
    a1, b1 = swap(a, "mp", 1), swap(b, "mp", 3)
    if first:
        a1, b1, *first = together(a1, b1, *first)
    else:
        _, b1 = together(a1, b1)
    a, b = add(a, a1), add(b, b1)
    loaded = load(a) if first else load(a, b)
    a2, b2, *rest = together(swap(a, "mp", 3), swap(b, "mp", 1), *second, *loaded)
    return (a, b, a2, b2), rest[len(second) :], first, rest[: len(second)]


def shards(inputs, cotangent, conv_kernels, point_weights):
    me = lax.axis_index("mp").astype(jnp.int32)[None]

    def weights(layer):
        def load(*after):
            *_, kernels, points = together(*after, conv_kernels, point_weights)
            return kernels[layer], points[layer]

        return load

    go, come = block_to_residue()
    sent = dot(go, jnp.concatenate([inputs, cotangent], axis=0)).astype(BF16)
    got = lax.all_to_all(sent.reshape(PEERS, 8, SHARD), "seq", 0, 0)
    own = dot(come, got.reshape(256, SHARD)).astype(BF16)
    own, cotangent = own[:ROWS], own[ROWS:]
    loaded = weights(0)(own)
    one, three, two, *loaded = together(*[swap(own, "mp", mask) for mask in (1, 3, 2)], *loaded)
    full, narrow, hid = struct((ROWS, C), BF16), struct((ROWS, H), F32), struct((ROWS, H), BF16)
    half = struct((ROWS, HALF), BF16)
    scratch = [pltpu.VMEM((ROWS, C), BF16)]
    x, inner, ta, tb = call(
        start_kernel,
        [full, narrow, half, half],
        scratch,
        (me, own, one, three, two, *loaded),
        {0: pltpu.SMEM},
    )
    saved = [(x, inner)]
    tables = {2: relative_order(Z, X), 1: relative_order(X, Z), 0: absolute_order()}
    tables[3] = tables[2]
    block_go, block_come = residue_to_block()
    for layer in (1, 2):
        second = []
        if layer == 1:
            cotangent, ta = together(cotangent, ta)
            second = [swap(cotangent, "mp", mask) for mask in (1, 3, 2)]
        terms, loaded, _, second = sum_mp(ta, tb, weights(layer), (), second)
        if layer == 1:
            parts = (me, cotangent, *second)
            (g,) = call(gather_kernel, [full], [], parts, {0: pltpu.SMEM}, flops=1e6)
        x, inner, ta, tb = call(
            functools.partial(forward_kernel, layer),
            [full, narrow, half, half],
            scratch,
            (x, *terms, *loaded),
        )
        saved.append((x, inner))
    terms, loaded, _, _ = sum_mp(ta, tb, weights(3))
    x, inner, inner_grad, ta, tb = call(
        functools.partial(turn_kernel, 3),
        [full, narrow, hid, half, half],
        scratch,
        (x, *terms, g, *loaded),
    )
    grad_b = g
    for layer in (3, 2, 1):
        keep, send = weight_terms(layer, tables[layer], inner_grad, inner, x, grad_b)
        first, second = [keep], [swap(send, "seq", 1)]
        if layer == 1:
            second = [*merge(keep, second[0], 2)]
        if layer == 1:
            three_kept, three_sent = halved(three_kept, three_got)
            second += [swap(three_sent, "seq", 24), swap(two_sent, "seq", 8)]
        if layer == 2:
            second += [swap(three_sent, "seq", 8)]
        terms, loaded, (keep,), (other, *rest) = sum_mp(ta, tb, weights(layer - 1), first, second)
        if layer > 1:
            kept, sent = merge(keep, other, 2)
        if layer == 3:
            three_kept, three_sent = kept, sent
        if layer == 2:
            (three_got,) = rest
            two_kept, two_sent = kept, sent
        if layer == 1:
            kept = other
            sent, three_got, two_got = rest
        above, (x, inner) = x, saved[layer - 1]
        if layer > 1:
            g, grad_b, inner_grad, ta, tb = call(
                functools.partial(backward_kernel, layer - 1),
                [struct((ROWS, C), F32), full, hid, half, half],
                [],
                (g, *terms, above, inner, *loaded),
            )
    two_kept, two_sent = halved(two_kept, two_got)
    piece, wide = struct((ROWS, SHARD), BF16), struct((ROWS, SHARD), F32)
    grad_b, inner_grad, own, *pieces, base, rate = call(
        final_kernel,
        [full, hid, wide, piece, piece, piece, wide, wide],
        [pltpu.VMEM((ROWS, C), F32), pltpu.VMEM((ROWS, C), F32)],
        (me, g, *terms, above, x, inner, *loaded),
        {0: pltpu.SMEM},
    )
    come = swap(sent, "seq", X)
    pieces = [swap(s, "mp", mask) for s, mask in zip(pieces, (1, 3, 2))]
    two_got = swap(two_sent, "seq", 3 * Z)
    keep, send = weight_terms(0, tables[0], inner_grad, inner, x, grad_b)
    other = swap(send, "seq", 1)
    mine, send = call(
        pack_kernel,
        [struct((16, C), BF16)] * 2,
        [],
        (own, *pieces, base, rate, block_go),
        flops=1e7,
    )
    late = [halved(two_kept, two_got), halved(three_kept, three_got)]
    late = [jnp.concatenate(parts, axis=0) for parts in zip(*late)]
    sibling = swap(send, "seq", 1)
    kept, sent = halved(kept, come)
    late_kept, late_sent = late
    first = call(
        exchange_kernel, [struct((16, 32, C), BF16)], [], (keep, other, mine, sibling), flops=1e7
    )[0]
    first = over_chips(first)
    come = swap(sent, "seq", 3 * X)
    late_come = swap(late_sent, "seq", X)
    late_kept, late_sent = (
        jnp.concatenate(
            [add(late_kept[n : n + 24], late_come[n : n + 24]) for n in (at, at + 48)], axis=0
        )
        for at in (0, 24)
    )
    late_come = swap(late_sent, "seq", 3 * X)
    kept, sent = halved(kept, come)
    come = swap(sent, "seq", Z)
    kept, sent = halved(kept, come)
    come = swap(sent, "seq", 3 * Z)
    gradient, kernel_grad, point_grad = call(
        sums_kernel,
        [wide, struct((3, 6, LAYERS, C), F32), struct((6, LAYERS, C), F32)],
        [],
        (first, kept, come, late_kept, late_come, block_come),
        flops=1e7,
    )
    return gradient, kernel_grad.transpose(2, 0, 1, 3), point_grad.transpose(1, 0, 2)


def solution(mesh):
    return jax.shard_map(
        shards,
        mesh=mesh,
        in_specs=(P("seq", "mp"), P("seq", "mp"), P(None, None, "mp", None), P(None, "mp", None)),
        out_specs=(
            P("seq", "mp"),
            P(None, None, ("mp", "seq"), None),
            P(None, ("mp", "seq"), None),
        ),
        check_vma=False,
    )
```

```python
import functools

import jax
import jax.numpy as jnp
import numpy as np
from jax import lax
from jax.experimental import pallas as pl
from jax.experimental.pallas import tpu as pltpu
from jax.sharding import PartitionSpec as P

LAYERS = 4
ROWS = 128
C = 1536
H = 192
HALF = C // 2
SHARD = C // 4
PEERS = 32
BF16 = jnp.bfloat16
F32 = jnp.float32
ORDER = (0, 3, 1, 2)
X, Z = 2, 8
ROOT = float(np.sqrt(2.0 / np.pi))
CUBE = 0.044715


def together(*values):
    return lax.optimization_barrier(values)


def dot(a, b, ca=1, cb=0):
    return lax.dot_general(a, b, (((ca,), (cb,)), ((), ())), preferred_element_type=F32)


def swap(values, axis, mask):
    peers = lax.axis_size(axis)
    return lax.ppermute(values, axis, [(i, i ^ mask) for i in range(peers)])


def add(a, b):
    return (a.astype(F32) + b.astype(F32)).astype(BF16)


def slope(x):
    square = x * x
    t = jnp.tanh(ROOT * x * (1.0 + CUBE * square))
    return 0.5 * (1.0 + t) + 0.5 * x * (1.0 - t * t) * (ROOT * (1.0 + 3.0 * CUBE * square))


def shifted(values, by):
    if by == 0:
        return values
    length = values.shape[0]
    zeros = jnp.zeros((abs(by),) + values.shape[1:], values.dtype)
    if by > 0:
        return jnp.concatenate([values[by:], zeros], axis=0)
    return jnp.concatenate([zeros, values[: length + by]], axis=0)


def struct(shape, kind):
    return jax.ShapeDtypeStruct(shape, kind)


def call(body, outs, scratch, args, spaces=None, flops=4e8):
    spaces = spaces or {}
    return pl.pallas_call(
        body,
        out_shape=outs,
        in_specs=[
            pl.BlockSpec(memory_space=spaces.get(i, pltpu.VMEM)) for i in range(len(args))
        ],
        out_specs=[pl.BlockSpec(memory_space=pltpu.VMEM)] * len(outs),
        scratch_shapes=scratch,
        compiler_params=pltpu.CompilerParams(vmem_limit_bytes=16 * 2**20),
        cost_estimate=pl.CostEstimate(flops=1000, bytes_accessed=1000, transcendentals=0),
    )(*args)


def chunks():
    return [slice(i, i + 16) for i in range(0, ROWS, 16)]


def total_of(rows, half, first, second):
    a, b = (first, second)[half]
    return a[rows].astype(F32) + b[rows].astype(F32)


def conv(active, k_mem, distance):
    taps = [dot(active, k_mem[k], 1, 1) for k in range(3)]
    return taps[1] + shifted(taps[0], -distance) + shifted(taps[2], distance)


def conv_back(inner_grad, k_mem, distance):
    out = None
    for k in range(3):
        moved = shifted(inner_grad, (1 - k) * distance).astype(BF16)
        part = dot(moved, k_mem[k])
        out = part if out is None else out + part
    return out


def put_halves(term, ta, tb):
    term = term.astype(BF16)
    ta[...] = term[:, :HALF]
    tb[...] = term[:, HALF:]


def backward_of(inner, grad_b, p_mem):
    hidden_grad = dot(grad_b, p_mem[...], 1, 1)
    return (hidden_grad * slope(inner)).astype(BF16)


def start_kernel(me, own, one, three, two, k_mem, p_mem, *rest):
    x, inner, ta, tb, active = rest
    for mask, block in ((0, own), (1, one), (3, three), (2, two)):
        at = pl.ds(pl.multiple_of((me[0] ^ mask) * SHARD, 128), SHARD)
        x[:, at] = block[...]
    for rows in chunks():
        active[rows] = jax.nn.gelu(x[rows].astype(F32)).astype(BF16)
    values = conv(active[...], k_mem, 1)
    inner[...] = values
    put_halves(dot(jax.nn.gelu(values).astype(BF16), p_mem[...]), ta, tb)


def gather_kernel(me, own, one, three, two, out):
    for mask, block in ((0, own), (1, one), (3, three), (2, two)):
        at = pl.ds(pl.multiple_of((me[0] ^ mask) * SHARD, 128), SHARD)
        out[:, at] = block[...]


def forward_kernel(layer, x, a, b, a2, b2, k_mem, p_mem, *rest):
    x1, inner, ta, tb, active = rest
    advance(x, a, b, a2, b2, x1, active)
    values = conv(active[...], k_mem, 2**layer)
    inner[...] = values
    put_halves(dot(jax.nn.gelu(values).astype(BF16), p_mem[...]), ta, tb)


def advance(x, a, b, a2, b2, x1, active):
    for rows in chunks():
        for half in (0, 1):
            at = slice(half * HALF, half * HALF + HALF)
            total = total_of(rows, half, (a, a2), (b, b2))
            values = (x[rows, at].astype(F32) + total).astype(BF16)
            x1[rows, at] = values
            active[rows, at] = jax.nn.gelu(values.astype(F32)).astype(BF16)


def turn_kernel(layer, x, a, b, a2, b2, g, k_mem, p_mem, *rest):
    x1, inner, inner_grad, ta, tb, active = rest
    advance(x, a, b, a2, b2, x1, active)
    before = conv(active[...], k_mem, 2**layer)
    inner[...] = before
    values = backward_of(before, g[...], p_mem)
    inner_grad[...] = values
    put_halves(conv_back(values.astype(F32), k_mem, 2**layer), ta, tb)


def retreat(g, a, b, a2, b2, x, g1, grad_b):
    for rows in chunks():
        for half in (0, 1):
            at = slice(half * HALF, half * HALF + HALF)
            total = total_of(rows, half, (a, a2), (b, b2))
            values = g[rows, at].astype(F32) + slope(x[rows, at].astype(F32)) * total
            g1[rows, at] = values
            grad_b[rows, at] = values.astype(BF16)


def backward_kernel(layer, g, a, b, a2, b2, x, inner, k_mem, p_mem, *rest):
    g1, grad_b, inner_grad, ta, tb = rest
    retreat(g, a, b, a2, b2, x, g1, grad_b)
    values = backward_of(inner[...], grad_b[...], p_mem)
    inner_grad[...] = values
    put_halves(conv_back(values.astype(F32), k_mem, 2**layer), ta, tb)


def final_kernel(me, g, a, b, a2, b2, x, first, inner, k_mem, p_mem, *rest):
    grad_b, inner_grad, own, one, three, two, base, rate, term, g1 = rest
    retreat(g, a, b, a2, b2, x, g1, grad_b)
    at = pl.ds(pl.multiple_of(me[0] * SHARD, 128), SHARD)
    rate[...] = slope(first[:, at].astype(F32))
    values = backward_of(inner[...], grad_b[...], p_mem)
    inner_grad[...] = values
    term[...] = conv_back(values.astype(F32), k_mem, 1)
    for mask, ref in ((0, own), (1, one), (3, three), (2, two)):
        at = pl.ds(pl.multiple_of((me[0] ^ mask) * SHARD, 128), SHARD)
        ref[...] = term[:, at].astype(ref.dtype)
    base[...] = g1[:, pl.ds(pl.multiple_of(me[0] * SHARD, 128), SHARD)]


def pack_kernel(own, one, three, two, base, rate, order, keep, send):
    total = own[...]
    for ref in (one, three, two):
        total = total + ref[...].astype(F32)
    values = (base[...] + rate[...] * total).astype(BF16)
    values = dot(order[...], values).astype(BF16)
    for part, ref in enumerate((keep, send)):
        for t in range(4):
            rows = slice(32 * t + 16 * part, 32 * t + 16 * part + 16)
            ref[:, t * SHARD : (t + 1) * SHARD] = values[rows]


def weight_kernel(distance, inner_grad, inner, x, grad_b, table, keep, send):
    grad = inner_grad[...].astype(F32)
    top = None
    for k in range(3):
        moved = shifted(grad, (1 - k) * distance).astype(BF16)
        part = dot(moved, table[k * H : (k + 1) * H])
        top = part if top is None else top + part
    bottom = dot(jax.nn.gelu(inner[...]).astype(BF16), table[3 * H :])
    left = jnp.concatenate([top, bottom], axis=0).T.astype(BF16)
    for column in range(0, C, 384):
        at = slice(column, column + 384)
        active = jax.nn.gelu(x[:, at].astype(F32)).astype(BF16)
        right = jnp.concatenate([active, grad_b[:, at]], axis=0)
        for ref, row in ((keep, 0), (send, 384)):
            ref[:, at] = dot(left[row : row + 384], right).astype(BF16)


def weight_terms(layer, table, inner_grad, inner, x, grad_b):
    body = functools.partial(weight_kernel, 2**layer)
    outs = [struct((384, C), BF16)] * 2
    return call(body, outs, [], (inner_grad, inner, x, grad_b, table), flops=8e8)


def merge_kernel(kept, other, *outs):
    size = outs[0].shape[0]
    for number, out in enumerate(outs):
        rows = slice(size * number, size * number + size)
        out[...] = add(kept[rows], other[rows])


def merge(kept, other, count):
    return call(
        merge_kernel, [struct((384 // count, C), BF16)] * count, [], (kept, other), flops=1e7
    )


def exchange_kernel(kept, other, mine, sibling, out):
    total = kept[...].astype(F32) + other[...].astype(F32)
    mine, sibling = mine[...].astype(F32), sibling[...].astype(F32)
    for chip in range(16):
        parts = [total[24 * chip : 24 * chip + 24], mine[chip : chip + 1], sibling[chip : chip + 1]]
        out[chip] = jnp.concatenate([*parts, jnp.zeros((6, C), F32)], axis=0).astype(BF16)


def sums_kernel(first, kept, come, late_kept, late_come, order, gradient, kernel_out, point_out):
    total = first[0].astype(F32)
    ends = [total[24:]]
    for i in range(1, 16):
        part = first[i].astype(F32)
        ends.append(part[24:])
        total = total + part
    ends = [jnp.concatenate([e[n : n + 1] for e in ends], axis=0) for n in (0, 1)]
    ends = jnp.concatenate(ends, axis=0).astype(BF16)
    for t in range(4):
        rows = slice(32 * t, 32 * t + 32)
        gradient[rows] = dot(order[...], ends[:, t * SHARD : (t + 1) * SHARD])
    second = kept[...].astype(F32) + come[...].astype(F32)
    late = late_kept[...].astype(F32) + late_come[...].astype(F32)
    layers = (total[:24], second, late[:24], late[24:])
    for row in range(24):
        values = jnp.concatenate([v[row : row + 1] for v in layers], axis=0)
        if row < 18:
            kernel_out[row // 6, row % 6] = values
        else:
            point_out[row - 18] = values


def table_of(source, columns):
    (source,) = together(jnp.asarray(source, jnp.int32))
    return (lax.broadcasted_iota(jnp.int32, (len(source), columns), 1) == source[:, None]).astype(
        BF16
    )


def by_source(blocks):
    column = np.arange(768)
    row = column % 24
    (source,) = together(jnp.asarray(row // 6 * H + row % 6, jnp.int32) + 6 * blocks)
    return (lax.broadcasted_iota(jnp.int32, (768, 768), 0) == source[None]).astype(BF16)


def absolute_order():
    core = lax.axis_index("seq") % 2
    block = np.arange(768) // 24
    return by_source(
        jnp.asarray(2 * (block % 16), jnp.int32) + (core ^ jnp.asarray(block // 16, jnp.int32))
    )


def relative_order(outer, inner):
    me = lax.axis_index("seq")
    masks = [c + outer * i + inner * j for c in (0, 1) for i in ORDER for j in ORDER]
    return by_source(me ^ jnp.asarray(np.repeat(masks, 24), jnp.int32))


def block_to_residue():
    n = np.arange(256)
    r, t = n // 8, n % 8
    go = t // 4 * 128 + t % 4 * 32 + r
    come = n % 128 // 4 * 8 + n // 128 * 4 + n % 4
    return table_of(go, 256), table_of(come, 256)


def residue_to_block():
    core = lax.axis_index("seq") % 2
    n = np.arange(32)
    device = jnp.asarray(2 * (n % 16), jnp.int32) + (core ^ jnp.asarray(n // 16, jnp.int32))
    go = (4 * device[None] + jnp.arange(4, dtype=jnp.int32)[:, None]).reshape(128)
    (go, device) = together(go, device)
    go = lax.broadcasted_iota(jnp.int32, (128, 128), 1) == go[:, None]
    come = lax.broadcasted_iota(jnp.int32, (32, 32), 0) == device[None]
    return go.astype(BF16), come.astype(BF16)


def halved(kept, come):
    rows = kept.shape[0] // 2
    return add(kept[:rows], come[:rows]), add(kept[rows:], come[rows:])


def over_chips(values):
    groups = [[2 * i + core for i in range(PEERS // 2)] for core in (0, 1)]
    return lax.all_to_all(values, "seq", 0, 0, axis_index_groups=groups)


def sum_mp(a, b, load, first=(), second=()):
    a1, b1 = swap(a, "mp", 1), swap(b, "mp", 3)
    if first:
        a1, b1, *first = together(a1, b1, *first)
    else:
        _, b1 = together(a1, b1)
    a, b = add(a, a1), add(b, b1)
    loaded = load(a) if first else load(a, b)
    a2, b2, *rest = together(swap(a, "mp", 3), swap(b, "mp", 1), *second, *loaded)
    return (a, b, a2, b2), rest[len(second) :], first, rest[: len(second)]


def shards(inputs, cotangent, conv_kernels, point_weights):
    me = lax.axis_index("mp").astype(jnp.int32)[None]

    def weights(layer):
        def load(*after):
            *_, kernels, points = together(*after, conv_kernels, point_weights)
            return kernels[layer], points[layer]

        return load

    go, come = block_to_residue()
    sent = dot(go, jnp.concatenate([inputs, cotangent], axis=0)).astype(BF16)
    got = lax.all_to_all(sent.reshape(PEERS, 8, SHARD), "seq", 0, 0)
    own = dot(come, got.reshape(256, SHARD)).astype(BF16)
    own, cotangent = own[:ROWS], own[ROWS:]
    loaded = weights(0)(own)
    one, three, two, *loaded = together(*[swap(own, "mp", mask) for mask in (1, 3, 2)], *loaded)
    full, narrow, hid = struct((ROWS, C), BF16), struct((ROWS, H), F32), struct((ROWS, H), BF16)
    half = struct((ROWS, HALF), BF16)
    scratch = [pltpu.VMEM((ROWS, C), BF16)]
    x, inner, ta, tb = call(
        start_kernel,
        [full, narrow, half, half],
        scratch,
        (me, own, one, three, two, *loaded),
        {0: pltpu.SMEM},
    )
    saved = [(x, inner)]
    tables = {2: relative_order(Z, X), 1: relative_order(X, Z), 0: absolute_order()}
    tables[3] = tables[2]
    block_go, block_come = residue_to_block()
    for layer in (1, 2):
        second = []
        if layer == 2:
            cotangent, ta = together(cotangent, ta)
            second = [swap(cotangent, "mp", mask) for mask in (1, 3, 2)]
        terms, loaded, _, second = sum_mp(ta, tb, weights(layer), (), second)
        if layer == 2:
            parts = (me, cotangent, *second)
            (g,) = call(gather_kernel, [full], [], parts, {0: pltpu.SMEM}, flops=1e6)
        x, inner, ta, tb = call(
            functools.partial(forward_kernel, layer),
            [full, narrow, half, half],
            scratch,
            (x, *terms, *loaded),
        )
        saved.append((x, inner))
    terms, loaded, _, _ = sum_mp(ta, tb, weights(3))
    x, inner, inner_grad, ta, tb = call(
        functools.partial(turn_kernel, 3),
        [full, narrow, hid, half, half],
        scratch,
        (x, *terms, g, *loaded),
    )
    grad_b = g
    for layer in (3, 2, 1):
        keep, send = weight_terms(layer, tables[layer], inner_grad, inner, x, grad_b)
        first, second = [keep], [swap(send, "seq", 1)]
        if layer == 1:
            second = [*merge(keep, second[0], 2)]
        if layer == 1:
            three_kept, three_sent = halved(three_kept, three_got)
            second += [swap(three_sent, "seq", 24), swap(two_sent, "seq", 8)]
        if layer == 2:
            second += [swap(three_sent, "seq", 8)]
        terms, loaded, (keep,), (other, *rest) = sum_mp(ta, tb, weights(layer - 1), first, second)
        if layer > 1:
            kept, sent = merge(keep, other, 2)
        if layer == 3:
            three_kept, three_sent = kept, sent
        if layer == 2:
            (three_got,) = rest
            two_kept, two_sent = kept, sent
        if layer == 1:
            kept = other
            sent, three_got, two_got = rest
        above, (x, inner) = x, saved[layer - 1]
        if layer > 1:
            g, grad_b, inner_grad, ta, tb = call(
                functools.partial(backward_kernel, layer - 1),
                [struct((ROWS, C), F32), full, hid, half, half],
                [],
                (g, *terms, above, inner, *loaded),
            )
    two_kept, two_sent = halved(two_kept, two_got)
    piece, wide = struct((ROWS, SHARD), BF16), struct((ROWS, SHARD), F32)
    grad_b, inner_grad, own, *pieces, base, rate = call(
        final_kernel,
        [full, hid, wide, piece, piece, piece, wide, wide],
        [pltpu.VMEM((ROWS, C), F32), pltpu.VMEM((ROWS, C), F32)],
        (me, g, *terms, above, x, inner, *loaded),
        {0: pltpu.SMEM},
    )
    come = swap(sent, "seq", X)
    pieces = [swap(s, "mp", mask) for s, mask in zip(pieces, (1, 3, 2))]
    two_got = swap(two_sent, "seq", 3 * Z)
    keep, send = weight_terms(0, tables[0], inner_grad, inner, x, grad_b)
    other = swap(send, "seq", 1)
    mine, send = call(
        pack_kernel,
        [struct((16, C), BF16)] * 2,
        [],
        (own, *pieces, base, rate, block_go),
        flops=1e7,
    )
    late = [halved(two_kept, two_got), halved(three_kept, three_got)]
    late = [jnp.concatenate(parts, axis=0) for parts in zip(*late)]
    sibling = swap(send, "seq", 1)
    kept, sent = halved(kept, come)
    late_kept, late_sent = late
    first = call(
        exchange_kernel, [struct((16, 32, C), BF16)], [], (keep, other, mine, sibling), flops=1e7
    )[0]
    first = over_chips(first)
    come = swap(sent, "seq", 3 * X)
    late_come = swap(late_sent, "seq", X)
    late_kept, late_sent = (
        jnp.concatenate(
            [add(late_kept[n : n + 24], late_come[n : n + 24]) for n in (at, at + 48)], axis=0
        )
        for at in (0, 24)
    )
    late_come = swap(late_sent, "seq", 3 * X)
    kept, sent = halved(kept, come)
    come = swap(sent, "seq", Z)
    kept, sent = halved(kept, come)
    come = swap(sent, "seq", 3 * Z)
    gradient, kernel_grad, point_grad = call(
        sums_kernel,
        [wide, struct((3, 6, LAYERS, C), F32), struct((6, LAYERS, C), F32)],
        [],
        (first, kept, come, late_kept, late_come, block_come),
        flops=1e7,
    )
    return gradient, kernel_grad.transpose(2, 0, 1, 3), point_grad.transpose(1, 0, 2)


def solution(mesh):
    return jax.shard_map(
        shards,
        mesh=mesh,
        in_specs=(P("seq", "mp"), P("seq", "mp"), P(None, None, "mp", None), P(None, "mp", None)),
        out_specs=(
            P("seq", "mp"),
            P(None, None, ("mp", "seq"), None),
            P(None, ("mp", "seq"), None),
        ),
        check_vma=False,
    )
```
